128 devices in a mesh: lag: 16 (over y, x_hi, core), src: 8 (over z, x_lo).
Axes of the slice: x: 4 (x_hi: 2, x_lo: 2; x = x_hi * 2 + x_lo), y: 4, z: 4, core: 2. Of those that a mesh axis runs over, the one named last changes fastest.
Arguments:
- reflection: bfloat16 [1024, 16, 2048], P(None, 'src', 'lag'), may hold values from -0.046875 to 0.046875
- focus_plus: bfloat16 [16, 8, 2048], P('src', None, 'lag'), may hold values from -6 to 6
- focus_start: bfloat16 [16, 8, 2048], P('src', None, 'lag'), may hold values from -6 to 6
- onset_receiver: int32 [1024, 8], replicated, may hold values from 128 to 1024, as said below
- onset_source: int32 [16, 8], P('src'), may hold values from 128 to 1024, as said below
Outputs:
- focus_minus: bfloat16 [1024, 8, 2048], P('src', None, 'lag')
- focus_next: float32 [16, 8, 2048], P('src', None, 'lag')
The draws below stay inside these ranges and needn't reach their ends.
Inputs may be any that keep to these rules, and one draw needn't show every extreme that they name: `onset_receiver`: onset of the direct arrival in samples from the middle of the time axis. `onset_source`: onset of the direct arrival in samples from the middle of the time axis.
All inputs are finite; a program needn't handle non-finite values.
Results may differ from the reference program's by a relative error of at most 0.012.
Values may be sent and summed in bfloat16 or wider, within the bound.
A program may use at most 128 MiB of HBM per device.

```python
import math
import jax
import jax.numpy as jnp
from jax import lax

RCV = 1024
NT = 2048
FOC = 8
SRCS = 16


def draw_onset_receiver(key, part):
    drawn = jax.random.randint(jax.random.fold_in(key, 11), (RCV, FOC), NT // 16, NT // 2 + 1, dtype=jnp.int32)
    drawn = drawn.at[0, 0].set(NT // 2)
    return drawn.at[RCV - 1, FOC - 1].set(NT // 16)


def draw_onset_source(key, part):
    drawn = jax.random.randint(jax.random.fold_in(key, 23), (SRCS, FOC), NT // 16, NT // 2 + 1, dtype=jnp.int32)
    drawn = drawn.at[0, 0].set(NT // 2)
    return drawn.at[SRCS - 1, FOC - 1].set(NT // 16)


def raised(entries, key, source, target, parts, factor):
    owner, partner = [(jnp.arange(entries.shape[axis_at]) // (entries.shape[axis_at] // parts)).reshape([-1 if axis == axis_at else 1 for axis in range(entries.ndim)]) for axis_at in (source, target)]
    chosen = jax.random.permutation(key, parts)[partner]
    strong = (owner == chosen) | (owner == (partner + parts // 2) % parts)
    return jnp.where(strong, factor * entries, entries)


def shard_levels(stream_key, extent, pieces, least, high):
    gain, own = 1.0, jax.random.fold_in(stream_key, 6)
    for dim, blocks in pieces:
        draws = jnp.exp(jax.random.uniform(jax.random.fold_in(own, dim), (blocks,), jnp.float32, least / len(pieces), high / len(pieces)))
        gain = gain * jnp.repeat(draws, extent[dim] // blocks).reshape([-1 if axis == dim else 1 for axis in range(len(extent))])
    return gain


def centred(stream_key, dims, spread, most, pieces=(), held_as=jnp.bfloat16):
    array = jax.random.normal(stream_key, dims, jnp.float32) * spread
    if len(pieces) > 0:
        array = shard_levels(stream_key, dims, pieces, -0.22, 0.18) * array
    return jnp.clip(array, min=-most, max=most).astype(held_as)


def gaussian_with(key, shape, deviation, limit, shards, heavy, held_as=jnp.bfloat16):
    result = deviation * jax.random.normal(key, shape, jnp.float32)
    if shards:
        result = result * shard_levels(key, shape, shards, -0.22, 0.18)
    return jnp.clip(raised(result, jax.random.fold_in(key, 3), *heavy), -limit, limit).astype(held_as)


def setup_inputs(seed: int = 0) -> dict:
    key_of = jax.random.split(jax.random.key(seed), 6)
    return {
        "reflection": gaussian_with(key_of[0], (RCV, SRCS, NT), (SRCS * NT) ** -0.5, 0.046875, ((1, 8), (2, 16)), (1, 0, 8, 2.0)),
        "focus_plus": centred(key_of[1], (SRCS, FOC, NT), 1.0, 6.0, ((0, 8), (2, 16))),
        "focus_start": centred(key_of[2], (SRCS, FOC, NT), 1.0, 6.0, ((0, 8), (2, 16))),
        "onset_receiver": draw_onset_receiver(jax.random.fold_in(key_of[5], 71), 0),
        "onset_source": draw_onset_source(jax.random.fold_in(key_of[5], 71), 0),
    }


def causal_window_mask(onset_index, length):
    sample_index = jnp.arange(length, dtype=jnp.int32)
    centre = length // 2
    lower_edge = centre - onset_index[..., None]
    upper_edge = centre - 1 + onset_index[..., None]
    inside = (sample_index >= lower_edge) & (sample_index <= upper_edge)
    return jnp.where(inside, 1.0, 0.0).astype(jnp.float32)


def reference(reflection, focus_plus, focus_start, onset_receiver, onset_source):
    padded_len = 2 * NT
    group_rows = math.gcd(RCV, 64)
    focus_hat = jnp.fft.rfft(focus_plus.astype(jnp.float32), n=padded_len, axis=-1)
    grouped = reflection.reshape(RCV // group_rows, group_rows, SRCS, NT)

    def forward_rows(data_rows):
        rows_hat = jnp.fft.rfft(data_rows.astype(jnp.float32), n=padded_len, axis=-1)
        matrix_product = jnp.einsum("csw,sfw->cfw", rows_hat, focus_hat, precision=lax.Precision.HIGHEST)
        return jnp.fft.irfft(matrix_product, n=padded_len, axis=-1)[..., :NT].astype(jnp.float32)

    upgoing = lax.map(forward_rows, grouped).reshape(RCV, FOC, NT)
    focus_minus = (causal_window_mask(onset_receiver, NT) * upgoing).astype(jnp.bfloat16)
    minus_grouped = focus_minus.reshape(RCV // group_rows, group_rows, FOC, NT)

    def backward_rows(running_sum, inputs):
        data_rows, minus_rows = inputs
        rows_hat = jnp.fft.rfft(data_rows.astype(jnp.float32), n=padded_len, axis=-1)
        minus_hat = jnp.fft.rfft(minus_rows.astype(jnp.float32), n=padded_len, axis=-1)
        matrix_product = jnp.einsum("csw,cfw->sfw", jnp.conj(rows_hat), minus_hat, precision=lax.Precision.HIGHEST)
        return running_sum + matrix_product, None

    running_sum, _ = lax.scan(backward_rows, jnp.zeros_like(focus_hat), (grouped, minus_grouped))
    correlation = jnp.fft.irfft(running_sum, n=padded_len, axis=-1)[..., :NT].astype(jnp.float32)
    focus_next = focus_start.astype(jnp.float32) + causal_window_mask(onset_source, NT) * correlation[..., ::-1]
    return focus_minus, focus_next
```

```python
import functools
import math

import jax
import jax.numpy as jnp
import numpy as np
from jax import lax
from jax.experimental import pallas as pl
from jax.experimental.pallas import tpu as pltpu
from jax.sharding import PartitionSpec as P

MESH = pl.DeviceIdType.MESH
LAGS, SRCS = 16, 8
J = 128
BLOCKS = 16
RADIX = 32
HALF = RADIX // 2 + 1
TOTAL = RADIX * J
F32, BF16 = jnp.float32, jnp.bfloat16


def add(a, b):
    if a is None or b is None:
        return b if a is None else a
    return a + b


def sub(a, b):
    if b is None:
        return a
    return -b if a is None else a - b


def neg(a):
    return None if a is None else -a


def scale(a, c):
    if a is None or c == 0.0:
        return None
    if c == 1.0:
        return a
    return -a if c == -1.0 else a * c


def root(n, k, sign):
    k = k % n
    if 4 * k % n == 0:
        c, s = [(1.0, 0.0), (0.0, 1.0), (-1.0, 0.0), (0.0, -1.0)][4 * k // n]
    else:
        c, s = math.cos(2 * math.pi * k / n), math.sin(2 * math.pi * k / n)
    return c, sign * s


def times(z, w):
    (re, im), (c, s) = z, w
    if re is not None and im is not None and abs(abs(c) - abs(s)) < 1e-12:
        h = abs(c)
        a, b = math.copysign(1.0, c), math.copysign(1.0, s)
        first = re if a > 0 else -re
        second = re if b > 0 else -re
        return (
            (first - im if b > 0 else first + im) * h,
            (second + im if a > 0 else second - im) * h,
        )
    return sub(scale(re, c), scale(im, s)), add(scale(re, s), scale(im, c))


def cadd(a, b):
    return add(a[0], b[0]), add(a[1], b[1])


def csub(a, b):
    return sub(a[0], b[0]), sub(a[1], b[1])


def cfft(values, sign):
    n = len(values)
    if n == 1:
        return values
    even, odd = cfft(values[0::2], sign), cfft(values[1::2], sign)
    odd = [times(v, root(n, k, sign)) for k, v in enumerate(odd)]
    return [cadd(a, b) for a, b in zip(even, odd)] + [csub(a, b) for a, b in zip(even, odd)]


def real_fft(x):
    n = len(x)
    if n == 1:
        return [(x[0], None)]
    half = n // 2
    z = [add(x[p], x[p + half]) for p in range(half)]
    d = [sub(x[p], x[p + half]) for p in range(half)]
    out = [None] * (half + 1)
    if n == 2:
        return [(z[0], None), (d[0], None)]
    out[0::2] = real_fft(z)
    quarter = n // 4
    turned = [times((d[p], neg(d[p + quarter])), root(n, p, -1)) for p in range(quarter)]
    for q, v in enumerate(cfft(turned, -1)):
        k = 4 * q + 1
        if k <= half:
            out[k] = v
        else:
            out[n - k] = (v[0], neg(v[1]))
    return out


def real_sum(spectrum):
    n = 2 * (len(spectrum) - 1)
    half = n // 2
    if n == 2:
        return [spectrum[0][0] + spectrum[1][0], spectrum[0][0] - spectrum[1][0]]
    even = real_sum(spectrum[0::2])
    quarter = n // 4
    terms = []
    for q in range(quarter):
        k = 4 * q + 1
        terms.append(spectrum[k] if k <= half else (spectrum[n - k][0], -spectrum[n - k][1]))
    turned = [times(v, root(n, p, 1)) for p, v in enumerate(cfft(terms, 1))]
    odd = [v[0] for v in turned] + [-v[1] for v in turned]
    if n == RADIX:
        return [even[p] + odd[p] for p in range(half)]
    return [even[p] + odd[p] for p in range(half)] + [even[p] - odd[p] for p in range(half)]


def split(matrix):
    high = matrix.astype(np.float32).astype(BF16)
    low = (matrix - high.astype(np.float64)).astype(np.float32).astype(BF16)
    return np.stack([high, low])


def as_real(matrix):
    return np.block([[matrix.real, matrix.imag], [-matrix.imag, matrix.real]])


@functools.cache
def tables():
    j = np.arange(J)
    k1 = np.arange(HALF)
    weight = np.where((k1 == 0) | (k1 == RADIX // 2), 1.0, 2.0)[:, None]
    forward = np.exp(-2j * np.pi * np.outer(j, j) / J)
    inverse = np.exp(2j * np.pi * np.outer(j, j) / J) / TOTAL
    turn = np.exp(-2j * np.pi * np.outer(k1, j) / TOTAL)
    back = weight * turn.conj()
    matrices = np.stack(
        [split(as_real(m)) for m in (forward, inverse, inverse[:, ::-1])]
    )
    turns = np.stack([np.stack([t.real, t.imag], 1) for t in (turn, back, back[:, ::-1])])
    return matrices, turns.reshape(3 * HALF * 2, J).astype(np.float32)


def turn_rows(turn_ref, which, k):
    at = (which * HALF + k) * 2
    return (
        jnp.broadcast_to(turn_ref[at : at + 1, :], (8, J)),
        jnp.broadcast_to(turn_ref[at + 1 : at + 2, :], (8, J)),
    )


def store_spectrum(turn_ref, blocks, ref, rows):
    for k, (re, im) in enumerate(real_fft(list(blocks) + [None] * (RADIX - BLOCKS))):
        if k == 0:
            im = jnp.zeros_like(re)
        else:
            c, s = turn_rows(turn_ref, 0, k)
            if im is None:
                re, im = re * c, re * s
            else:
                re, im = re * c - im * s, re * s + im * c
        ref[k, rows, 0:J] = re
        ref[k, rows, J : 2 * J] = im


def load_blocks(turn_ref, which, ref, rows):
    spectrum = []
    for k in range(HALF):
        re, im = ref[k, rows, 0:J], ref[k, rows, J : 2 * J]
        if k == 0:
            spectrum.append((re, None))
            continue
        c, s = turn_rows(turn_ref, which, k)
        if k == RADIX // 2:
            spectrum.append((re * c - im * s, None))
        else:
            spectrum.append((re * c - im * s, re * s + im * c))
    return real_sum(spectrum)


def product(a, mat_ref, which):
    high = a.astype(BF16)
    low = (a - high.astype(F32)).astype(BF16)
    dot = functools.partial(jnp.dot, preferred_element_type=F32)
    return dot(high, mat_ref[which, 0]) + dot(low, mat_ref[which, 0]) + dot(high, mat_ref[which, 1])


def row_of(r, s):
    return (s // 2) * 16 + r * 2 + s % 2


def local_kernel(refl_ref, plus_ref, onset_ref, mat_ref, turn_ref, minus_ref, corr_ref, a_ref, h_ref, u_ref, c_ref):
    def spectra(g, carry):
        for source, base in ((refl_ref, 0), (plus_ref, 128)):
            values = [source[g, p].astype(F32) for p in range(BLOCKS)]
            for half in range(2):
                rows = pl.ds(pl.multiple_of(base + 16 * g + 8 * half, 8), 8)
                store_spectrum(turn_ref, [v[8 * half : 8 * half + 8] for v in values], a_ref, rows)
        return carry

    lax.fori_loop(0, SRCS, spectra, 0)

    def forward(k, carry):
        h_ref[k] = product(a_ref[k], mat_ref, 0)
        for first in range(0, 8, 4):
            acc = [None] * 4
            for s in range(16):
                at = 128 + 8 * s
                fr, fi = h_ref[k, at : at + 8, 0:J], h_ref[k, at : at + 8, J : 2 * J]
                for i in range(4):
                    row = row_of(first + i, s)
                    rr = jnp.broadcast_to(h_ref[k, row : row + 1, 0:J], (8, J))
                    ri = jnp.broadcast_to(h_ref[k, row : row + 1, J : 2 * J], (8, J))
                    term = (rr * fr - ri * fi, rr * fi + ri * fr)
                    acc[i] = term if acc[i] is None else cadd(acc[i], term)
            for i in range(4):
                at = 8 * (first + i)
                u_ref[k, at : at + 8, 0:J] = acc[i][0]
                u_ref[k, at : at + 8, J : 2 * J] = acc[i][1]
        u_ref[k] = product(u_ref[k], mat_ref, 1)
        return carry

    lax.fori_loop(0, HALF, forward, 0)

    sample = lax.broadcasted_iota(jnp.int32, (8, J), 1)

    def middle(pair, carry):
        kept = []
        for half in range(2):
            rows = pl.ds(pl.multiple_of(16 * pair + 8 * half, 8), 8)
            onset = onset_ref[rows, :]
            low, high = BLOCKS * J // 2 - onset, BLOCKS * J // 2 - 1 + onset
            blocks = []
            for p, x in enumerate(load_blocks(turn_ref, 1, u_ref, rows)):
                n = sample + p * J
                x = jnp.where((n >= low) & (n <= high), x, 0.0)
                blocks.append(x.astype(BF16).astype(F32))
            kept.append(blocks)
            store_spectrum(turn_ref, blocks, a_ref, rows)
        for p in range(BLOCKS):
            both = jnp.concatenate([kept[0][p], kept[1][p]], axis=0).astype(BF16)
            minus_ref[p, pl.ds(pl.multiple_of(16 * pair, 16), 16), :] = both
        return carry

    lax.fori_loop(0, 4, middle, 0)

    def backward(k, carry):
        u_ref[k] = product(a_ref[k, 0:64], mat_ref, 0)
        for first in range(0, 16, 4):
            acc = [None] * 4
            for r in range(8):
                mr, mi = u_ref[k, 8 * r : 8 * r + 8, 0:J], u_ref[k, 8 * r : 8 * r + 8, J : 2 * J]
                for i in range(4):
                    row = row_of(r, first + i)
                    rr = jnp.broadcast_to(h_ref[k, row : row + 1, 0:J], (8, J))
                    ri = jnp.broadcast_to(h_ref[k, row : row + 1, J : 2 * J], (8, J))
                    term = (rr * mr + ri * mi, rr * mi - ri * mr)
                    acc[i] = term if acc[i] is None else cadd(acc[i], term)
            for i in range(4):
                at = 8 * (first + i)
                c_ref[k, at : at + 8, 0:J] = acc[i][0]
                c_ref[k, at : at + 8, J : 2 * J] = acc[i][1]
        c_ref[k] = product(c_ref[k], mat_ref, 2)
        return carry

    lax.fori_loop(0, HALF, backward, 0)

    def last(g, carry):
        kept = []
        for half in range(2):
            rows = pl.ds(pl.multiple_of(16 * g + 8 * half, 8), 8)
            kept.append(load_blocks(turn_ref, 2, c_ref, rows))
        for p in range(BLOCKS):
            both = jnp.concatenate([kept[0][BLOCKS - 1 - p], kept[1][BLOCKS - 1 - p]], axis=0)
            corr_ref[g, p] = both.astype(BF16)
        return carry

    lax.fori_loop(0, SRCS, last, 0)


def position():
    return lax.axis_index("lag"), lax.axis_index("src")


def partner(i, my_lag, my_src):
    return (my_lag + i // SRCS) % LAGS, (my_src + i % SRCS) % SRCS


def greet(barrier, my_lag, my_src):
    def signal(i, carry):
        pl.semaphore_signal(barrier, inc=1, device_id=partner(i, my_lag, my_src), device_id_type=MESH)
        return carry

    lax.fori_loop(1, LAGS * SRCS, signal, 0)
    pl.semaphore_wait(barrier, LAGS * SRCS - 1)


def spread_kernel(refl_ref, plus_ref, refl_out, plus_out, sems):
    my_lag, my_src = position()
    chip, core = my_lag // 2, my_lag % 2
    greet(pltpu.get_barrier_semaphore(), my_lag, my_src)

    def remote(source, target, send, recv, where):
        pltpu.make_async_remote_copy(
            src_ref=source, dst_ref=target, send_sem=sems.at[send], recv_sem=sems.at[recv],
            device_id=where, device_id_type=MESH,
        ).start()

    for i in range(1, SRCS):
        remote(plus_ref, plus_out.at[my_src, chip, core], 2, 3, (my_lag, (my_src + i) % SRCS))
    pltpu.make_async_copy(plus_ref, plus_out.at[my_src, chip, core], sems.at[3]).start()

    def send(i, carry):
        lag, src = partner(i, my_lag, my_src)
        remote(refl_ref.at[src, lag], refl_out.at[my_src, my_lag], 0, 1, (lag, src))
        return carry

    lax.fori_loop(1, LAGS * SRCS, send, 0)
    pltpu.make_async_copy(refl_ref.at[my_src, my_lag], refl_out.at[my_src, my_lag], sems.at[1]).start()

    def wait(ref, sem):
        pltpu.make_async_copy(ref, ref, sems.at[sem]).wait()

    wait(plus_out.at[:, chip, core], 3)
    mine = plus_out.at[:, chip, core]
    for i in range(1, LAGS // 2):
        remote(mine, mine, 4, 5, ((my_lag + 2 * i) % LAGS, my_src))
    wait(plus_out.at[:, pl.ds(0, 7), 0], 5)
    half = plus_out.at[:, :, core]
    remote(half, half, 6, 7, (chip * 2 + 1 - core, my_src))
    wait(half, 7)
    wait(refl_out, 1)
    wait(plus_out.at[pl.ds(0, 7), 0, 0], 2)
    wait(plus_out.at[:, pl.ds(0, 7), 0], 4)
    wait(half, 6)
    wait(refl_out.at[pl.ds(0, 127 // 16 * 1)], 0)
    wait(refl_out.at[0, pl.ds(0, 15)], 0)


def gather_kernel(minus_ref, corr_ref, start_ref, onset_ref, minus_out, next_out, parts, sems):
    my_lag, my_src = position()
    greet(pltpu.get_barrier_semaphore(), my_lag, my_src)

    def remote(source, target, send, recv, where):
        pltpu.make_async_remote_copy(
            src_ref=source, dst_ref=target, send_sem=sems.at[send], recv_sem=sems.at[recv],
            device_id=where, device_id_type=MESH,
        ).start()

    for i in range(1, LAGS):
        lag = (my_lag + i) % LAGS
        remote(minus_ref.at[lag], minus_out.at[my_lag], 2, 3, (lag, my_src))
    pltpu.make_async_copy(minus_ref.at[my_lag], minus_out.at[my_lag], sems.at[3]).start()

    def send(i, carry):
        lag, src = partner(i, my_lag, my_src)
        remote(corr_ref.at[src, lag], parts.at[my_src, my_lag], 0, 1, (lag, src))
        return carry

    lax.fori_loop(1, LAGS * SRCS, send, 0)
    pltpu.make_async_copy(corr_ref.at[my_src, my_lag], parts.at[my_src, my_lag], sems.at[1]).start()

    def wait(ref, sem):
        pltpu.make_async_copy(ref, ref, sems.at[sem]).wait()

    wait(parts, 1)
    total = jnp.zeros((16, J), F32)
    for g in range(SRCS):
        for l in range(LAGS):
            total = total + parts[g, l].astype(F32)
    n = lax.broadcasted_iota(jnp.int32, (16, J), 1) + my_lag * J
    onset = onset_ref[...]
    inside = (n >= BLOCKS * J // 2 - onset) & (n <= BLOCKS * J // 2 - 1 + onset)
    next_out[...] = start_ref[...].astype(F32) + jnp.where(inside, total, 0.0)
    wait(minus_out, 3)
    wait(minus_out.at[pl.ds(0, 15)], 2)
    wait(parts.at[pl.ds(0, 7)], 0)
    wait(parts.at[0, pl.ds(0, 15)], 0)


def body(reflection, focus_plus, focus_start, onset_receiver, onset_source):
    vmem = pl.BlockSpec(memory_space=pltpu.VMEM)
    share = lax.axis_index("src") * 128 + lax.axis_index("lag") * 8
    onset = lax.dynamic_slice_in_dim(onset_receiver, share, 8, 0)
    onset = jnp.broadcast_to(onset.reshape(64, 1), (64, J))
    onset_s = jnp.broadcast_to(onset_source.reshape(16, 1), (16, J))
    matrices, turns = tables()

    refl, plus = pl.pallas_call(
        spread_kernel,
        out_shape=(
            jax.ShapeDtypeStruct((SRCS, LAGS, 16, J), BF16),
            jax.ShapeDtypeStruct((SRCS, LAGS // 2, 2, 16, J), BF16),
        ),
        in_specs=[vmem, vmem],
        out_specs=(vmem, vmem),
        scratch_shapes=[pltpu.SemaphoreType.DMA((8,))],
        compiler_params=pltpu.CompilerParams(
            collective_id=0, has_side_effects=True, vmem_limit_bytes=32 * 2**20
        ),
        name="spread",
    )(reflection.reshape(SRCS, LAGS, 16, J), focus_plus.reshape(16, J))

    minus, corr = pl.pallas_call(
        local_kernel,
        out_shape=(
            jax.ShapeDtypeStruct((BLOCKS, 64, J), BF16),
            jax.ShapeDtypeStruct((SRCS, LAGS, 16, J), BF16),
        ),
        in_specs=[vmem] * 5,
        out_specs=(vmem, vmem),
        scratch_shapes=[
            pltpu.VMEM((HALF, 256, 2 * J), F32),
            pltpu.VMEM((HALF, 256, 2 * J), F32),
            pltpu.VMEM((HALF, 64, 2 * J), F32),
            pltpu.VMEM((HALF, 128, 2 * J), F32),
        ],
        compiler_params=pltpu.CompilerParams(vmem_limit_bytes=48 * 2**20),
        name="local",
    )(refl, plus.reshape(SRCS, LAGS, 16, J), onset, jnp.asarray(matrices), jnp.asarray(turns))

    minus_out, next_out = pl.pallas_call(
        gather_kernel,
        out_shape=(
            jax.ShapeDtypeStruct((LAGS, 64, J), BF16),
            jax.ShapeDtypeStruct((16, J), F32),
        ),
        in_specs=[vmem] * 4,
        out_specs=(vmem, vmem),
        scratch_shapes=[pltpu.VMEM((SRCS, LAGS, 16, J), BF16), pltpu.SemaphoreType.DMA((4,))],
        compiler_params=pltpu.CompilerParams(
            collective_id=1, has_side_effects=True, vmem_limit_bytes=32 * 2**20
        ),
        name="collect",
    )(minus, corr, focus_start.reshape(16, J), onset_s)
    return minus_out.reshape(128, 8, J), next_out.reshape(2, 8, J)


def solution(mesh):
    return jax.shard_map(
        body,
        mesh=mesh,
        in_specs=(
            P(None, "src", "lag"),
            P("src", None, "lag"),
            P("src", None, "lag"),
            P(),
            P("src", None),
        ),
        out_specs=(P("src", None, "lag"), P("src", None, "lag")),
        check_vma=False,
    )
```

```python
import functools
import math

import jax
import jax.numpy as jnp
import numpy as np
from jax import lax
from jax.experimental import pallas as pl
from jax.experimental.pallas import tpu as pltpu
from jax.sharding import PartitionSpec as P

MESH = pl.DeviceIdType.MESH
LAGS, SRCS = 16, 8
CHIPS = LAGS // 2
RCV = 8
J = 128
BLOCKS = 16
RADIX = 32
HALF = RADIX // 2 + 1
TOTAL = RADIX * J
F32, BF16 = jnp.float32, jnp.bfloat16


def add(a, b):
    if a is None or b is None:
        return b if a is None else a
    return a + b


def sub(a, b):
    if b is None:
        return a
    return -b if a is None else a - b


def neg(a):
    return None if a is None else -a


def scale(a, c):
    if a is None or c == 0.0:
        return None
    if c == 1.0:
        return a
    return -a if c == -1.0 else a * c


def root(n, k, sign):
    k = k % n
    if 4 * k % n == 0:
        c, s = [(1.0, 0.0), (0.0, 1.0), (-1.0, 0.0), (0.0, -1.0)][4 * k // n]
    else:
        c, s = math.cos(2 * math.pi * k / n), math.sin(2 * math.pi * k / n)
    return c, sign * s


def times(z, w):
    (re, im), (c, s) = z, w
    if re is not None and im is not None and abs(abs(c) - abs(s)) < 1e-12:
        h = abs(c)
        a, b = math.copysign(1.0, c), math.copysign(1.0, s)
        first = re if a > 0 else -re
        second = re if b > 0 else -re
        return (
            (first - im if b > 0 else first + im) * h,
            (second + im if a > 0 else second - im) * h,
        )
    return sub(scale(re, c), scale(im, s)), add(scale(re, s), scale(im, c))


def cadd(a, b):
    return add(a[0], b[0]), add(a[1], b[1])


def csub(a, b):
    return sub(a[0], b[0]), sub(a[1], b[1])


def cfft(values, sign):
    n = len(values)
    if n == 1:
        return values
    even, odd = cfft(values[0::2], sign), cfft(values[1::2], sign)
    odd = [times(v, root(n, k, sign)) for k, v in enumerate(odd)]
    return [cadd(a, b) for a, b in zip(even, odd)] + [csub(a, b) for a, b in zip(even, odd)]


def real_fft(x):
    n = len(x)
    if n == 1:
        return [(x[0], None)]
    half = n // 2
    z = [add(x[p], x[p + half]) for p in range(half)]
    d = [sub(x[p], x[p + half]) for p in range(half)]
    out = [None] * (half + 1)
    if n == 2:
        return [(z[0], None), (d[0], None)]
    out[0::2] = real_fft(z)
    quarter = n // 4
    turned = [times((d[p], neg(d[p + quarter])), root(n, p, -1)) for p in range(quarter)]
    for q, v in enumerate(cfft(turned, -1)):
        k = 4 * q + 1
        if k <= half:
            out[k] = v
        else:
            out[n - k] = (v[0], neg(v[1]))
    return out


def real_sum(spectrum):
    n = 2 * (len(spectrum) - 1)
    half = n // 2
    if n == 2:
        return [spectrum[0][0] + spectrum[1][0], spectrum[0][0] - spectrum[1][0]]
    even = real_sum(spectrum[0::2])
    quarter = n // 4
    terms = []
    for q in range(quarter):
        k = 4 * q + 1
        terms.append(spectrum[k] if k <= half else (spectrum[n - k][0], -spectrum[n - k][1]))
    turned = [times(v, root(n, p, 1)) for p, v in enumerate(cfft(terms, 1))]
    odd = [v[0] for v in turned] + [-v[1] for v in turned]
    if n == RADIX:
        return [even[p] + odd[p] for p in range(half)]
    return [even[p] + odd[p] for p in range(half)] + [even[p] - odd[p] for p in range(half)]


def split(matrix):
    high = matrix.astype(np.float32).astype(BF16)
    low = (matrix - high.astype(np.float64)).astype(np.float32).astype(BF16)
    return np.stack([high, low])


def as_real(matrix):
    return np.block([[matrix.real, matrix.imag], [-matrix.imag, matrix.real]])


@functools.cache
def tables():
    j = np.arange(J)
    k1 = np.arange(HALF)
    weight = np.where((k1 == 0) | (k1 == RADIX // 2), 1.0, 2.0)[:, None]
    forward = np.exp(-2j * np.pi * np.outer(j, j) / J)
    inverse = np.exp(2j * np.pi * np.outer(j, j) / J) / TOTAL
    turn = np.exp(-2j * np.pi * np.outer(k1, j) / TOTAL)
    back = weight * turn.conj()
    matrices = np.stack(
        [split(as_real(m)) for m in (forward, inverse, inverse[:, ::-1])]
    )
    turns = np.stack([np.stack([t.real, t.imag], 1) for t in (turn, back, back[:, ::-1])])
    return matrices, turns.reshape(3 * HALF * 2, J).astype(np.float32)


def turn_rows(turn_ref, which, k):
    at = (which * HALF + k) * 2
    return (
        jnp.broadcast_to(turn_ref[at : at + 1, :], (8, J)),
        jnp.broadcast_to(turn_ref[at + 1 : at + 2, :], (8, J)),
    )


def store_spectrum(turn_ref, blocks, ref, rows):
    for k, (re, im) in enumerate(real_fft(list(blocks) + [None] * (RADIX - BLOCKS))):
        if k == 0:
            im = jnp.zeros_like(re)
        else:
            c, s = turn_rows(turn_ref, 0, k)
            if im is None:
                re, im = re * c, re * s
            else:
                re, im = re * c - im * s, re * s + im * c
        ref[k, rows, 0:J] = re
        ref[k, rows, J : 2 * J] = im


def load_blocks(turn_ref, which, ref, rows):
    spectrum = []
    for k in range(HALF):
        re, im = ref[k, rows, 0:J], ref[k, rows, J : 2 * J]
        if k == 0:
            spectrum.append((re, None))
            continue
        c, s = turn_rows(turn_ref, which, k)
        if k == RADIX // 2:
            spectrum.append((re * c - im * s, None))
        else:
            spectrum.append((re * c - im * s, re * s + im * c))
    return real_sum(spectrum)


def product(a, mat_ref, which):
    shape = a.shape
    a = a.reshape(shape[0] * shape[1], 2 * J)
    high = a.astype(BF16)
    low = (a - high.astype(F32)).astype(BF16)
    dot = functools.partial(jnp.dot, preferred_element_type=F32)
    out = dot(high, mat_ref[which, 0]) + dot(low, mat_ref[which, 0]) + dot(high, mat_ref[which, 1])
    return out.reshape(shape)


def transform(tile, a_ref, out_ref, mat_ref, turn_ref):
    values = [tile(p).astype(F32) for p in range(BLOCKS)]
    for half in range(2):
        rows = slice(8 * half, 8 * half + 8)
        store_spectrum(turn_ref, [v[rows] for v in values], a_ref, rows)
    out_ref[...] = product(a_ref[...], mat_ref, 0)


def both(ref, k, row):
    return (
        jnp.broadcast_to(ref[k, row : row + 1, 0:J], (8, J)),
        jnp.broadcast_to(ref[k, row : row + 1, J : 2 * J], (8, J)),
    )


def forward_terms(refl, plus, u_ref):
    def step(k, carry):
        f = [(plus[k, 8 * s : 8 * s + 8, 0:J], plus[k, 8 * s : 8 * s + 8, J : 2 * J]) for s in range(2)]
        for r in range(RCV):
            rows = slice(8 * r, 8 * r + 8)
            re, im = u_ref[k, rows, 0:J], u_ref[k, rows, J : 2 * J]
            for s in range(2):
                rr, ri = both(refl, k, 2 * r + s)
                fr, fi = f[s]
                re, im = re + (rr * fr - ri * fi), im + (rr * fi + ri * fr)
            u_ref[k, rows, 0:J] = re
            u_ref[k, rows, J : 2 * J] = im
        return carry

    lax.fori_loop(0, HALF, step, 0, unroll=True)


def backward_terms(refl, m_ref, c_ref):
    def step(k, carry):
        acc = [None, None]
        for r in range(RCV):
            rows = slice(8 * r, 8 * r + 8)
            mr, mi = m_ref[k, rows, 0:J], m_ref[k, rows, J : 2 * J]
            for s in range(2):
                rr, ri = both(refl, k, 2 * r + s)
                term = (rr * mr + ri * mi, rr * mi - ri * mr)
                acc[s] = term if acc[s] is None else cadd(acc[s], term)
        for s in range(2):
            c_ref[k, 8 * s : 8 * s + 8, 0:J] = acc[s][0]
            c_ref[k, 8 * s : 8 * s + 8, J : 2 * J] = acc[s][1]
        return carry

    lax.fori_loop(0, HALF, step, 0, unroll=True)


def window(onset, sample):
    return (sample >= BLOCKS * J // 2 - onset) & (sample <= BLOCKS * J // 2 - 1 + onset)


def middle(u_ref, a_ref, onset_ref, first, turn_ref, minus_ref):
    lane = lax.broadcasted_iota(jnp.int32, (8, J), 1)

    def step(pair, carry):
        kept = []
        for half in range(2):
            at = 2 * pair + half
            rows = pl.ds(pl.multiple_of(8 * at, 8), 8)
            mine = jnp.where(lane == first + at, onset_ref[...], 0).astype(F32)
            onset = jnp.broadcast_to(jnp.sum(mine, axis=1, keepdims=True), (8, J)).astype(jnp.int32)
            blocks = []
            for p, x in enumerate(load_blocks(turn_ref, 1, u_ref, rows)):
                blocks.append(jnp.where(window(onset, lane + p * J), x, 0.0).astype(BF16).astype(F32))
            kept.append(blocks)
            store_spectrum(turn_ref, blocks, a_ref, rows)
        for p in range(BLOCKS):
            joined = jnp.concatenate([kept[0][p], kept[1][p]], axis=0).astype(BF16)
            minus_ref[p, pl.ds(pl.multiple_of(16 * pair, 16), 16), :] = joined
        return carry

    lax.fori_loop(0, RCV // 2, step, 0)


def kernel(
    refl_ref, plus_ref, start_ref, onset_r_ref, onset_s_ref, mat_hbm, turn_hbm,
    minus_out, next_out,
    refl, plus, mats, turns, onset_r, onset_s, start,
    a_ref, hr_ref, hf_ref, u_ref, b_ref, m_ref, c_ref,
    minus, corr, peer, chip_sum, parts,
    local_sem, one_sem, refl_sem, peer_sem,
):
    my_lag, my_src = lax.axis_index("lag"), lax.axis_index("src")
    chip, core = lax.div(my_lag, 2), lax.rem(my_lag, 2)

    def remote(source, target, send, recv, where):
        pltpu.make_async_remote_copy(
            src_ref=source, dst_ref=target, send_sem=send, recv_sem=recv, device_id=where, device_id_type=MESH
        ).start()

    def wait(ref, sem):
        pltpu.make_async_copy(ref, ref, sem).wait()

    loads = [
        (mat_hbm, mats), (turn_hbm, turns), (start_ref, start), (onset_s_ref, onset_s),
        (onset_r_ref.at[:, pl.ds(pl.multiple_of(my_src * J, J), J)], onset_r),
    ]
    loads = [pltpu.make_async_copy(a, b, local_sem.at[i]) for i, (a, b) in enumerate(loads)]
    for load in loads:
        load.start()

    barrier = pltpu.get_barrier_semaphore()

    def lag_at(i):
        return lax.rem(my_lag + i, LAGS)

    def src_at(d):
        return lax.rem(my_src + d, SRCS)

    def greet(lag, src):
        pl.semaphore_signal(barrier, inc=1, device_id=(lag, src), device_id_type=MESH)

    def greet_group(d, carry):
        for i in range(LAGS):
            greet(lag_at(i), src_at(d))
        return carry

    for i in range(1, LAGS):
        greet(lag_at(i), my_src)
    lax.fori_loop(1, SRCS, greet_group, 0)
    pl.semaphore_wait(barrier, LAGS * SRCS - 1)

    s_f1, r_f1, s_f2, r_f2, s_f3, r_f3, s_r, s_m, r_m, s_p, s_c, r_c = [one_sem.at[i] for i in range(12)]
    own = plus.at[my_src, chip, core]
    for d in range(1, SRCS):
        remote(plus_ref, own, s_f1, r_f1, (my_lag, src_at(d)))
    pltpu.make_async_copy(plus_ref, own, r_f1).start()

    def send_reflection(lag, src):
        remote(refl_ref.at[src, lag], refl.at[my_src, my_lag], s_r, refl_sem.at[my_src], (lag, src))

    for i in range(1, LAGS):
        send_reflection(lag_at(i), my_src)
    pltpu.make_async_copy(refl_ref.at[my_src, my_lag], refl.at[my_src, my_lag], refl_sem.at[my_src]).start()

    column = plus.at[:, chip, core]
    wait(column, r_f1)
    for i in range(1, CHIPS):
        remote(column, column, s_f2, r_f2, (lag_at(2 * i), my_src))

    def send_group(d, carry):
        for i in range(LAGS):
            send_reflection(lag_at(i), src_at(d))
        return carry

    lax.fori_loop(1, SRCS, send_group, 0)
    wait(plus.at[:, pl.ds(0, CHIPS - 1), 0], r_f2)
    half = plus.at[:, :, core]
    other = chip * 2 + 1 - core
    remote(half, half, s_f3, r_f3, (other, my_src))
    for load in loads:
        load.wait()
    u_ref[...] = jnp.zeros_like(u_ref)
    wait(half, r_f3)

    def plus_spectra(g, carry):
        transform(lambda p: plus[g, p // 2, p % 2], a_ref, hf_ref.at[g], mats, turns)
        return carry

    lax.fori_loop(0, SRCS, plus_spectra, 0)

    def forward(d, carry):
        g = lax.rem(my_src + SRCS - d, SRCS)
        wait(refl.at[g], refl_sem.at[g])
        transform(lambda p: refl[g, p], a_ref, hr_ref.at[g], mats, turns)
        forward_terms(hr_ref.at[g], hf_ref.at[g], u_ref)
        return carry

    lax.fori_loop(0, SRCS, forward, 0)
    u_ref[...] = product(u_ref[...], mats, 1)
    middle(u_ref, b_ref, onset_r, RCV * my_lag, turns, minus)

    for i in range(1, LAGS):
        remote(minus.at[lag_at(i)], minus_out.at[my_lag], s_m, r_m, (lag_at(i), my_src))
    pltpu.make_async_copy(minus.at[my_lag], minus_out.at[my_lag], r_m).start()
    m_ref[...] = product(b_ref[...], mats, 0)

    def add_and_send(d):
        g = src_at(d)
        wait(peer.at[g], peer_sem.at[g])
        chip_sum[g] = (corr[g, core].astype(F32) + peer[g].astype(F32)).astype(BF16)
        for i in range(CHIPS):
            to = lax.rem(chip + i, CHIPS)
            remote(chip_sum.at[g, to], parts.at[my_src, chip], s_c, r_c, (to * 2 + core, g))

    def backward(d, carry):
        g = src_at(d)
        backward_terms(hr_ref.at[g], m_ref, c_ref)
        c_ref[...] = product(c_ref[...], mats, 2)
        kept = [load_blocks(turns, 2, c_ref, slice(8 * h, 8 * h + 8)) for h in range(2)]
        for p in range(BLOCKS):
            at = BLOCKS - 1 - p
            corr[g, p % 2, p // 2] = jnp.concatenate([kept[0][at], kept[1][at]], axis=0).astype(BF16)
        remote(corr.at[g, 1 - core], peer.at[g], s_p, peer_sem.at[g], (other, my_src))
        pl.when(d > 1)(lambda: add_and_send(d - 1))
        return carry

    lax.fori_loop(1, SRCS + 1, backward, 0)
    g = my_src
    wait(peer.at[g], peer_sem.at[g])
    chip_sum[g] = (corr[g, core].astype(F32) + peer[g].astype(F32)).astype(BF16)
    for i in range(1, CHIPS):
        to = lax.rem(chip + i, CHIPS)
        remote(chip_sum.at[g, to], parts.at[my_src, chip], s_c, r_c, (to * 2 + core, g))
    pltpu.make_async_copy(chip_sum.at[g, chip], parts.at[my_src, chip], r_c).start()

    lane = lax.broadcasted_iota(jnp.int32, (8, J), 1)
    masks = []
    for s in range(2):
        row = jnp.broadcast_to(onset_s[s : s + 1, :], (8, 8)).astype(F32)
        pick = lax.broadcasted_iota(jnp.int32, (8, 8), 0) == lax.broadcasted_iota(jnp.int32, (8, 8), 1)
        onset = jnp.sum(jnp.where(pick, row, 0.0), axis=1, keepdims=True)
        masks.append(window(jnp.broadcast_to(onset, (8, J)).astype(jnp.int32), lane + my_lag * J))
    wait(parts, r_c)
    total = jnp.zeros((16, J), F32)
    for g in range(SRCS):
        for l in range(CHIPS):
            total = total + parts[g, l].astype(F32)
    begin = start[...].astype(F32)
    for s in range(2):
        rows = slice(8 * s, 8 * s + 8)
        next_out[rows, :] = begin[rows] + jnp.where(masks[s], total[rows], 0.0)

    wait(minus_out, r_m)
    wait(plus.at[pl.ds(0, SRCS - 1), 0, 0], s_f1)
    wait(plus.at[:, pl.ds(0, CHIPS - 1), 0], s_f2)
    wait(half, s_f3)
    wait(refl.at[pl.ds(0, SRCS - 1)], s_r)
    wait(refl.at[0, pl.ds(0, LAGS - 1)], s_r)
    wait(minus_out.at[pl.ds(0, LAGS - 1)], s_m)
    wait(peer, s_p)
    wait(parts.at[pl.ds(0, SRCS - 1)], s_c)
    wait(parts.at[0, pl.ds(0, CHIPS - 1)], s_c)


def body(reflection, focus_plus, focus_start, onset_receiver, onset_source):
    anywhere = pl.BlockSpec(memory_space=pl.ANY)
    vmem = pl.BlockSpec(memory_space=pltpu.VMEM)
    matrices, turns = tables()
    spectra = pltpu.VMEM((SRCS, HALF, 16, 2 * J), F32)
    tiles = pltpu.VMEM((SRCS, CHIPS, 16, J), BF16)
    minus_out, next_out = pl.pallas_call(
        kernel,
        out_shape=(
            jax.ShapeDtypeStruct((LAGS, 8 * RCV, J), BF16),
            jax.ShapeDtypeStruct((16, J), F32),
        ),
        in_specs=[anywhere] * 7,
        out_specs=(vmem, vmem),
        scratch_shapes=[
            pltpu.VMEM((SRCS, LAGS, 16, J), BF16),
            pltpu.VMEM((SRCS, CHIPS, 2, 16, J), BF16),
            pltpu.VMEM(matrices.shape, BF16),
            pltpu.VMEM(turns.shape, F32),
            pltpu.VMEM((8, J), jnp.int32),
            pltpu.VMEM((2, 8), jnp.int32),
            pltpu.VMEM((16, J), BF16),
            pltpu.VMEM((HALF, 16, 2 * J), F32),
            spectra,
            spectra,
            pltpu.VMEM((HALF, 64, 2 * J), F32),
            pltpu.VMEM((HALF, 64, 2 * J), F32),
            pltpu.VMEM((HALF, 64, 2 * J), F32),
            pltpu.VMEM((HALF, 16, 2 * J), F32),
            pltpu.VMEM((LAGS, 8 * RCV, J), BF16),
            pltpu.VMEM((SRCS, 2, CHIPS, 16, J), BF16),
            tiles,
            tiles,
            tiles,
            pltpu.SemaphoreType.DMA((5,)),
            pltpu.SemaphoreType.DMA((12,)),
            pltpu.SemaphoreType.DMA((SRCS,)),
            pltpu.SemaphoreType.DMA((SRCS,)),
        ],
        compiler_params=pltpu.CompilerParams(
            collective_id=0, has_side_effects=True, vmem_limit_bytes=60 * 2**20
        ),
        name="focus",
    )(
        reflection.reshape(SRCS, LAGS, 16, J),
        focus_plus.reshape(16, J),
        focus_start.reshape(16, J),
        onset_receiver.T,
        onset_source,
        jnp.asarray(matrices),
        jnp.asarray(turns),
    )
    return minus_out.reshape(J, 8, J), next_out.reshape(2, 8, J)


def solution(mesh):
    return jax.shard_map(
        body,
        mesh=mesh,
        in_specs=(
            P(None, "src", "lag"),
            P("src", None, "lag"),
            P("src", None, "lag"),
            P(),
            P("src", None),
        ),
        out_specs=(P("src", None, "lag"), P("src", None, "lag")),
        check_vma=False,
    )
```

```python
import functools
import math

import jax
import jax.numpy as jnp
import numpy as np
from jax import lax
from jax.experimental import pallas as pl
from jax.experimental.pallas import tpu as pltpu
from jax.sharding import PartitionSpec as P

MESH = pl.DeviceIdType.MESH
LAGS, SRCS = 16, 8
CHIPS = LAGS // 2
RCV = 8
EARLY = 5
DEPTH = 2
J = 128
BLOCKS = 16
RADIX = 32
HALF = RADIX // 2 + 1
TOTAL = RADIX * J
F32, BF16 = jnp.float32, jnp.bfloat16


def add(a, b):
    if a is None or b is None:
        return b if a is None else a
    return a + b


def sub(a, b):
    if b is None:
        return a
    return -b if a is None else a - b


def neg(a):
    return None if a is None else -a


def scale(a, c):
    if a is None or c == 0.0:
        return None
    if c == 1.0:
        return a
    return -a if c == -1.0 else a * c


def root(n, k, sign):
    k = k % n
    if 4 * k % n == 0:
        c, s = [(1.0, 0.0), (0.0, 1.0), (-1.0, 0.0), (0.0, -1.0)][4 * k // n]
    else:
        c, s = math.cos(2 * math.pi * k / n), math.sin(2 * math.pi * k / n)
    return c, sign * s


def times(z, w):
    (re, im), (c, s) = z, w
    if re is not None and im is not None and abs(abs(c) - abs(s)) < 1e-12:
        h = abs(c)
        a, b = math.copysign(1.0, c), math.copysign(1.0, s)
        first = re if a > 0 else -re
        second = re if b > 0 else -re
        return (
            (first - im if b > 0 else first + im) * h,
            (second + im if a > 0 else second - im) * h,
        )
    return sub(scale(re, c), scale(im, s)), add(scale(re, s), scale(im, c))


def cadd(a, b):
    return add(a[0], b[0]), add(a[1], b[1])


def csub(a, b):
    return sub(a[0], b[0]), sub(a[1], b[1])


def cfft(values, sign):
    n = len(values)
    if n == 1:
        return values
    even, odd = cfft(values[0::2], sign), cfft(values[1::2], sign)
    odd = [times(v, root(n, k, sign)) for k, v in enumerate(odd)]
    return [cadd(a, b) for a, b in zip(even, odd)] + [csub(a, b) for a, b in zip(even, odd)]


def real_fft(x):
    n = len(x)
    if n == 1:
        return [(x[0], None)]
    half = n // 2
    z = [add(x[p], x[p + half]) for p in range(half)]
    d = [sub(x[p], x[p + half]) for p in range(half)]
    out = [None] * (half + 1)
    if n == 2:
        return [(z[0], None), (d[0], None)]
    out[0::2] = real_fft(z)
    quarter = n // 4
    turned = [times((d[p], neg(d[p + quarter])), root(n, p, -1)) for p in range(quarter)]
    for q, v in enumerate(cfft(turned, -1)):
        k = 4 * q + 1
        if k <= half:
            out[k] = v
        else:
            out[n - k] = (v[0], neg(v[1]))
    return out


def real_sum(spectrum):
    n = 2 * (len(spectrum) - 1)
    half = n // 2
    if n == 2:
        return [spectrum[0][0] + spectrum[1][0], spectrum[0][0] - spectrum[1][0]]
    even = real_sum(spectrum[0::2])
    quarter = n // 4
    terms = []
    for q in range(quarter):
        k = 4 * q + 1
        terms.append(spectrum[k] if k <= half else (spectrum[n - k][0], -spectrum[n - k][1]))
    turned = [times(v, root(n, p, 1)) for p, v in enumerate(cfft(terms, 1))]
    odd = [v[0] for v in turned] + [-v[1] for v in turned]
    if n == RADIX:
        return [even[p] + odd[p] for p in range(half)]
    return [even[p] + odd[p] for p in range(half)] + [even[p] - odd[p] for p in range(half)]


def split(matrix):
    high = matrix.astype(np.float32).astype(BF16)
    low = (matrix - high.astype(np.float64)).astype(np.float32).astype(BF16)
    return np.stack([high, low])


def as_real(matrix):
    return np.block([[matrix.real, matrix.imag], [-matrix.imag, matrix.real]])


@functools.cache
def tables():
    j = np.arange(J)
    k1 = np.arange(HALF)
    weight = np.where((k1 == 0) | (k1 == RADIX // 2), 1.0, 2.0)[:, None]
    forward = np.exp(-2j * np.pi * np.outer(j, j) / J)
    inverse = np.exp(2j * np.pi * np.outer(j, j) / J) / TOTAL
    turn = np.exp(-2j * np.pi * np.outer(k1, j) / TOTAL)
    back = weight * turn.conj()
    matrices = np.stack(
        [split(as_real(m)) for m in (forward, inverse, inverse[:, ::-1])]
    )
    turns = np.stack([np.stack([t.real, t.imag], 1) for t in (turn, back, back[:, ::-1])])
    return matrices, turns.reshape(3 * HALF * 2, J).astype(np.float32)


def turn_rows(turn_ref, which, k):
    at = (which * HALF + k) * 2
    return (
        jnp.broadcast_to(turn_ref[at : at + 1, :], (8, J)),
        jnp.broadcast_to(turn_ref[at + 1 : at + 2, :], (8, J)),
    )


def store_spectrum(turn_ref, blocks, ref, rows):
    for k, (re, im) in enumerate(real_fft(list(blocks) + [None] * (RADIX - BLOCKS))):
        if k == 0:
            im = jnp.zeros_like(re)
        else:
            c, s = turn_rows(turn_ref, 0, k)
            if im is None:
                re, im = re * c, re * s
            else:
                re, im = re * c - im * s, re * s + im * c
        ref[k, rows, 0:J] = re
        ref[k, rows, J : 2 * J] = im


def load_blocks(turn_ref, which, ref, rows):
    spectrum = []
    for k in range(HALF):
        re, im = ref[k, rows, 0:J], ref[k, rows, J : 2 * J]
        if k == 0:
            spectrum.append((re, None))
            continue
        c, s = turn_rows(turn_ref, which, k)
        if k == RADIX // 2:
            spectrum.append((re * c - im * s, None))
        else:
            spectrum.append((re * c - im * s, re * s + im * c))
    return real_sum(spectrum)


def product(a, mat_ref, which):
    shape = a.shape
    a = a.reshape(shape[0] * shape[1], 2 * J)
    high = a.astype(BF16)
    low = (a - high.astype(F32)).astype(BF16)
    dot = functools.partial(jnp.dot, preferred_element_type=F32)
    out = dot(high, mat_ref[which, 0]) + dot(low, mat_ref[which, 0]) + dot(high, mat_ref[which, 1])
    return out.reshape(shape)


def transform(tile, a_ref, out_ref, mat_ref, turn_ref):
    values = [tile(p).astype(F32) for p in range(BLOCKS)]
    for half in range(2):
        rows = slice(8 * half, 8 * half + 8)
        store_spectrum(turn_ref, [v[rows] for v in values], a_ref, rows)
    out_ref[...] = product(a_ref[...], mat_ref, 0)


def both(ref, k, row):
    return (
        jnp.broadcast_to(ref[k, row : row + 1, 0:J], (8, J)),
        jnp.broadcast_to(ref[k, row : row + 1, J : 2 * J], (8, J)),
    )


def forward_terms(refl, plus, u_ref):
    def step(k, carry):
        f = [(plus[k, 8 * s : 8 * s + 8, 0:J], plus[k, 8 * s : 8 * s + 8, J : 2 * J]) for s in range(2)]
        for r in range(RCV):
            rows = slice(8 * r, 8 * r + 8)
            re, im = u_ref[k, rows, 0:J], u_ref[k, rows, J : 2 * J]
            for s in range(2):
                rr, ri = both(refl, k, 2 * r + s)
                fr, fi = f[s]
                re, im = re + (rr * fr - ri * fi), im + (rr * fi + ri * fr)
            u_ref[k, rows, 0:J] = re
            u_ref[k, rows, J : 2 * J] = im
        return carry

    lax.fori_loop(0, HALF, step, 0, unroll=True)


def backward_terms(refl, m_ref, c_ref):
    def step(k, carry):
        acc = [None, None]
        for r in range(RCV):
            rows = slice(8 * r, 8 * r + 8)
            mr, mi = m_ref[k, rows, 0:J], m_ref[k, rows, J : 2 * J]
            for s in range(2):
                rr, ri = both(refl, k, 2 * r + s)
                term = (rr * mr + ri * mi, rr * mi - ri * mr)
                acc[s] = term if acc[s] is None else cadd(acc[s], term)
        for s in range(2):
            c_ref[k, 8 * s : 8 * s + 8, 0:J] = acc[s][0]
            c_ref[k, 8 * s : 8 * s + 8, J : 2 * J] = acc[s][1]
        return carry

    lax.fori_loop(0, HALF, step, 0, unroll=True)


def window(onset, sample):
    return (sample >= BLOCKS * J // 2 - onset) & (sample <= BLOCKS * J // 2 - 1 + onset)


def middle(u_ref, a_ref, onset_ref, first, turn_ref, minus_ref):
    lane = lax.broadcasted_iota(jnp.int32, (8, J), 1)

    def step(pair, carry):
        kept = []
        for half in range(2):
            at = 2 * pair + half
            rows = pl.ds(pl.multiple_of(8 * at, 8), 8)
            mine = jnp.where(lane == first + at, onset_ref[...], 0).astype(F32)
            onset = jnp.broadcast_to(jnp.sum(mine, axis=1, keepdims=True), (8, J)).astype(jnp.int32)
            blocks = []
            for p, x in enumerate(load_blocks(turn_ref, 1, u_ref, rows)):
                blocks.append(jnp.where(window(onset, lane + p * J), x, 0.0).astype(BF16).astype(F32))
            kept.append(blocks)
            store_spectrum(turn_ref, blocks, a_ref, rows)
        for p in range(BLOCKS):
            joined = jnp.concatenate([kept[0][p], kept[1][p]], axis=0).astype(BF16)
            minus_ref[p, pl.ds(pl.multiple_of(16 * pair, 16), 16), :] = joined
        return carry

    lax.fori_loop(0, RCV // 2, step, 0)


def kernel(
    refl_ref, plus_ref, start_ref, onset_r_ref, onset_s_ref, mat_hbm, turn_hbm,
    minus_out, next_out,
    refl, plus, mats, turns, onset_r, onset_s, start,
    a_ref, hr_ref, hf_ref, u_ref, b_ref, m_ref, c_ref,
    minus, corr, peer, chip_sum, parts, own_parts,
    local_sem, one_sem, refl_sem, peer_sem,
):
    my_lag, my_src = lax.axis_index("lag"), lax.axis_index("src")
    chip, core = lax.div(my_lag, 2), lax.rem(my_lag, 2)

    def remote(source, target, send, recv, where):
        pltpu.make_async_remote_copy(
            src_ref=source, dst_ref=target, send_sem=send, recv_sem=recv, device_id=where, device_id_type=MESH
        ).start()

    def wait(ref, sem):
        pltpu.make_async_copy(ref, ref, sem).wait()

    loads = [
        (mat_hbm, mats), (turn_hbm, turns), (start_ref, start), (onset_s_ref, onset_s),
        (onset_r_ref.at[:, pl.ds(pl.multiple_of(my_src * J, J), J)], onset_r),
    ]
    loads = [pltpu.make_async_copy(a, b, local_sem.at[i]) for i, (a, b) in enumerate(loads)]
    for load in loads:
        load.start()

    barrier = pltpu.get_barrier_semaphore()

    def lag_at(i):
        return lax.rem(my_lag + i, LAGS)

    def src_at(d):
        return lax.rem(my_src + d, SRCS)

    def greet(lag, src):
        pl.semaphore_signal(barrier, inc=1, device_id=(lag, src), device_id_type=MESH)

    def greet_group(d, carry):
        for i in range(LAGS):
            greet(lag_at(i), src_at(d))
        return carry

    for i in range(1, LAGS):
        greet(lag_at(i), my_src)
    lax.fori_loop(1, SRCS, greet_group, 0)
    pl.semaphore_wait(barrier, LAGS * SRCS - 1)

    s_f, r_f, s_f2, r_f2, s_r, s_m, r_m, s_p, s_c, r_c, s_o, r_o = [one_sem.at[i] for i in range(12)]

    own = plus.at[core, my_src, chip]

    def same_core(i):
        return lax.rem(chip + i, CHIPS) * 2 + core

    def send_plus(d, carry):
        for i in range(CHIPS):
            remote(plus_ref, own, s_f, r_f, (same_core(i), src_at(d)))
        return carry

    def send_reflection(lag, src):
        remote(refl_ref.at[src, lag], refl.at[my_src, my_lag], s_r, refl_sem.at[my_src], (lag, src))

    def send_group(d, carry):
        for i in range(LAGS):
            send_reflection(lag_at(i), src_at(d))
        return carry

    for i in range(1, CHIPS):
        remote(plus_ref, own, s_f, r_f, (same_core(i), my_src))
    pltpu.make_async_copy(plus_ref, own, r_f).start()
    lax.fori_loop(1, SRCS, send_plus, 0)
    for i in range(1, LAGS):
        send_reflection(lag_at(i), my_src)
    pltpu.make_async_copy(refl_ref.at[my_src, my_lag], refl.at[my_src, my_lag], refl_sem.at[my_src]).start()
    lax.fori_loop(1, EARLY, send_group, 0)
    half = plus.at[core]
    other = chip * 2 + 1 - core
    wait(half, r_f)
    remote(half, half, s_f2, r_f2, (other, my_src))
    lax.fori_loop(EARLY, SRCS, send_group, 0)
    for load in loads:
        load.wait()
    u_ref[...] = jnp.zeros_like(u_ref)
    wait(half, r_f2)

    def plus_spectra(g, carry):
        transform(lambda p: plus[p % 2, g, p // 2], a_ref, hf_ref.at[g], mats, turns)
        return carry

    lax.fori_loop(0, SRCS, plus_spectra, 0)

    def forward(d, carry):
        g = lax.rem(my_src + SRCS - d, SRCS)
        wait(refl.at[g], refl_sem.at[g])
        transform(lambda p: refl[g, p], a_ref, hr_ref.at[g], mats, turns)
        forward_terms(hr_ref.at[g], hf_ref.at[g], u_ref)
        return carry

    lax.fori_loop(0, SRCS, forward, 0)
    u_ref[...] = product(u_ref[...], mats, 1)
    middle(u_ref, b_ref, onset_r, RCV * my_lag, turns, minus)

    def send_minus(i):
        remote(minus.at[lag_at(i)], minus_out.at[my_lag], s_m, r_m, (lag_at(i), my_src))

    pltpu.make_async_copy(minus.at[my_lag], minus_out.at[my_lag], r_m).start()
    for i in range(1, LAGS):
        send_minus(i)
    m_ref[...] = product(b_ref[...], mats, 0)

    def send_own():
        for i in range(1, LAGS):
            lag = lag_at(i)
            remote(corr.at[my_src, lax.rem(lag, 2), lax.div(lag, 2)], own_parts.at[my_lag], s_o, r_o, (lag, my_src))

    def add_and_send(g):
        wait(peer.at[g], peer_sem.at[g])
        chip_sum[g] = (corr[g, core].astype(F32) + peer[g].astype(F32)).astype(BF16)
        for i in range(CHIPS):
            to = lax.rem(chip + i, CHIPS)
            remote(chip_sum.at[g, to], parts.at[my_src, chip], s_c, r_c, (to * 2 + core, g))

    def backward(d, carry):
        g = src_at(d)
        backward_terms(hr_ref.at[g], m_ref, c_ref)
        c_ref[...] = product(c_ref[...], mats, 2)
        kept = [load_blocks(turns, 2, c_ref, slice(8 * h, 8 * h + 8)) for h in range(2)]
        for p in range(BLOCKS):
            at = BLOCKS - 1 - p
            corr[g, p % 2, p // 2] = jnp.concatenate([kept[0][at], kept[1][at]], axis=0).astype(BF16)

        @pl.when(d < SRCS)
        def _():
            remote(corr.at[g, 1 - core], peer.at[g], s_p, peer_sem.at[g], (other, my_src))

        pl.when(d == SRCS)(send_own)
        pl.when(d > DEPTH)(lambda: add_and_send(src_at(d - DEPTH)))
        return carry

    lax.fori_loop(1, SRCS + 1, backward, 0)
    for d in range(SRCS + 1 - DEPTH, SRCS):
        add_and_send(src_at(d))
    pltpu.make_async_copy(corr.at[my_src, core, chip], own_parts.at[my_lag], r_o).start()

    lane = lax.broadcasted_iota(jnp.int32, (8, J), 1)
    masks = []
    for s in range(2):
        row = jnp.broadcast_to(onset_s[s : s + 1, :], (8, 8)).astype(F32)
        pick = lax.broadcasted_iota(jnp.int32, (8, 8), 0) == lax.broadcasted_iota(jnp.int32, (8, 8), 1)
        onset = jnp.sum(jnp.where(pick, row, 0.0), axis=1, keepdims=True)
        masks.append(window(jnp.broadcast_to(onset, (8, J)).astype(jnp.int32), lane + my_lag * J))
    begin = start[...].astype(F32)
    wait(parts.at[pl.ds(0, SRCS - 1)], r_c)
    sums = [None] * 4
    for d in range(1, SRCS):
        for l in range(CHIPS):
            sums[l % 4] = add(sums[l % 4], parts[src_at(d), l].astype(F32))
    wait(own_parts, r_o)
    for l in range(LAGS):
        sums[l % 4] = add(sums[l % 4], own_parts[l].astype(F32))
    total = (sums[0] + sums[1]) + (sums[2] + sums[3])
    for s in range(2):
        rows = slice(8 * s, 8 * s + 8)
        next_out[rows, :] = begin[rows] + jnp.where(masks[s], total[rows], 0.0)

    wait(minus_out, r_m)
    wait(half.at[pl.ds(0, SRCS - 1)], s_f)
    wait(half.at[0, pl.ds(0, CHIPS - 1)], s_f)
    wait(half, s_f2)
    wait(refl.at[pl.ds(0, SRCS - 1)], s_r)
    wait(refl.at[0, pl.ds(0, LAGS - 1)], s_r)
    wait(minus_out.at[pl.ds(0, LAGS - 1)], s_m)
    wait(peer.at[pl.ds(0, SRCS - 1)], s_p)
    wait(parts.at[pl.ds(0, SRCS - 1)], s_c)
    wait(own_parts.at[pl.ds(0, LAGS - 1)], s_o)


def finish_kernel(minus_ref, next_ref, minus_out, next_out):
    minus_out[...] = minus_ref[...]
    next_out[...] = next_ref[...]


def body(reflection, focus_plus, focus_start, onset_receiver, onset_source):
    vmem = pl.BlockSpec(memory_space=pltpu.VMEM)
    matrices, turns = tables()
    spectra = pltpu.VMEM((SRCS, HALF, 16, 2 * J), F32)
    tiles = pltpu.VMEM((SRCS, CHIPS, 16, J), BF16)
    minus_out, next_out = pl.pallas_call(
        kernel,
        out_shape=(
            jax.ShapeDtypeStruct((LAGS, 8 * RCV, J), BF16),
            jax.ShapeDtypeStruct((16, J), F32),
        ),
        in_specs=[pl.BlockSpec(memory_space=pl.ANY)] * 7,
        out_specs=(vmem, vmem),
        scratch_shapes=[
            pltpu.VMEM((SRCS, LAGS, 16, J), BF16),
            pltpu.VMEM((2, SRCS, CHIPS, 16, J), BF16),
            pltpu.VMEM(matrices.shape, BF16),
            pltpu.VMEM(turns.shape, F32),
            pltpu.VMEM((8, J), jnp.int32),
            pltpu.VMEM((2, 8), jnp.int32),
            pltpu.VMEM((16, J), BF16),
            pltpu.VMEM((HALF, 16, 2 * J), F32),
            spectra,
            spectra,
            pltpu.VMEM((HALF, 64, 2 * J), F32),
            pltpu.VMEM((HALF, 64, 2 * J), F32),
            pltpu.VMEM((HALF, 64, 2 * J), F32),
            pltpu.VMEM((HALF, 16, 2 * J), F32),
            pltpu.VMEM((LAGS, 8 * RCV, J), BF16),
            pltpu.VMEM((SRCS, 2, CHIPS, 16, J), BF16),
            tiles,
            tiles,
            tiles,
            pltpu.VMEM((LAGS, 16, J), BF16),
            pltpu.SemaphoreType.DMA((5,)),
            pltpu.SemaphoreType.DMA((12,)),
            pltpu.SemaphoreType.DMA((SRCS,)),
            pltpu.SemaphoreType.DMA((SRCS,)),
        ],
        compiler_params=pltpu.CompilerParams(
            collective_id=0, has_side_effects=True, vmem_limit_bytes=60 * 2**20
        ),
        name="focus",
    )(
        reflection.reshape(SRCS, LAGS, 16, J),
        focus_plus.reshape(16, J),
        focus_start.reshape(16, J),
        onset_receiver.T,
        onset_source,
        jnp.asarray(matrices),
        jnp.asarray(turns),
    )
    minus_out, next_out = pl.pallas_call(
        finish_kernel,
        out_shape=(
            jax.ShapeDtypeStruct(minus_out.shape, BF16),
            jax.ShapeDtypeStruct(next_out.shape, F32),
        ),
        in_specs=[vmem] * 2,
        out_specs=(vmem, vmem),
        name="finish",
    )(minus_out, next_out)
    return minus_out.reshape(J, 8, J), next_out.reshape(2, 8, J)


def solution(mesh):
    return jax.shard_map(
        body,
        mesh=mesh,
        in_specs=(
            P(None, "src", "lag"),
            P("src", None, "lag"),
            P("src", None, "lag"),
            P(),
            P("src", None),
        ),
        out_specs=(P("src", None, "lag"), P("src", None, "lag")),
        check_vma=False,
    )
```

```python
import functools
import math

import jax
import jax.numpy as jnp
import numpy as np
from jax import lax
from jax.experimental import pallas as pl
from jax.experimental.pallas import tpu as pltpu
from jax.sharding import PartitionSpec as P

MESH = pl.DeviceIdType.MESH
LAGS, SRCS = 16, 8
CHIPS = LAGS // 2
RCV = 8
EARLY = 5
DEPTH = 2
AHEAD = 2
J = 128
BLOCKS = 16
RADIX = 32
HALF = RADIX // 2 + 1
TOTAL = RADIX * J
F32, BF16 = jnp.float32, jnp.bfloat16


def add(a, b):
    if a is None or b is None:
        return b if a is None else a
    return a + b


def sub(a, b):
    if b is None:
        return a
    return -b if a is None else a - b


def neg(a):
    return None if a is None else -a


def scale(a, c):
    if a is None or c == 0.0:
        return None
    if c == 1.0:
        return a
    return -a if c == -1.0 else a * c


def root(n, k, sign):
    k = k % n
    if 4 * k % n == 0:
        c, s = [(1.0, 0.0), (0.0, 1.0), (-1.0, 0.0), (0.0, -1.0)][4 * k // n]
    else:
        c, s = math.cos(2 * math.pi * k / n), math.sin(2 * math.pi * k / n)
    return c, sign * s


def times(z, w):
    (re, im), (c, s) = z, w
    if re is not None and im is not None and abs(abs(c) - abs(s)) < 1e-12:
        h = abs(c)
        a, b = math.copysign(1.0, c), math.copysign(1.0, s)
        first = re if a > 0 else -re
        second = re if b > 0 else -re
        return (
            (first - im if b > 0 else first + im) * h,
            (second + im if a > 0 else second - im) * h,
        )
    return sub(scale(re, c), scale(im, s)), add(scale(re, s), scale(im, c))


def cadd(a, b):
    return add(a[0], b[0]), add(a[1], b[1])


def csub(a, b):
    return sub(a[0], b[0]), sub(a[1], b[1])


def cfft(values, sign):
    n = len(values)
    if n == 1:
        return values
    even, odd = cfft(values[0::2], sign), cfft(values[1::2], sign)
    odd = [times(v, root(n, k, sign)) for k, v in enumerate(odd)]
    return [cadd(a, b) for a, b in zip(even, odd)] + [csub(a, b) for a, b in zip(even, odd)]


def real_fft(x):
    n = len(x)
    if n == 1:
        return [(x[0], None)]
    half = n // 2
    z = [add(x[p], x[p + half]) for p in range(half)]
    d = [sub(x[p], x[p + half]) for p in range(half)]
    out = [None] * (half + 1)
    if n == 2:
        return [(z[0], None), (d[0], None)]
    out[0::2] = real_fft(z)
    quarter = n // 4
    turned = [times((d[p], neg(d[p + quarter])), root(n, p, -1)) for p in range(quarter)]
    for q, v in enumerate(cfft(turned, -1)):
        k = 4 * q + 1
        if k <= half:
            out[k] = v
        else:
            out[n - k] = (v[0], neg(v[1]))
    return out


def real_sum(spectrum):
    n = 2 * (len(spectrum) - 1)
    half = n // 2
    if n == 2:
        return [spectrum[0][0] + spectrum[1][0], spectrum[0][0] - spectrum[1][0]]
    even = real_sum(spectrum[0::2])
    quarter = n // 4
    terms = []
    for q in range(quarter):
        k = 4 * q + 1
        terms.append(spectrum[k] if k <= half else (spectrum[n - k][0], -spectrum[n - k][1]))
    turned = [times(v, root(n, p, 1)) for p, v in enumerate(cfft(terms, 1))]
    odd = [v[0] for v in turned] + [-v[1] for v in turned]
    if n == RADIX:
        return [even[p] + odd[p] for p in range(half)]
    return [even[p] + odd[p] for p in range(half)] + [even[p] - odd[p] for p in range(half)]


def split(matrix):
    high = matrix.astype(np.float32).astype(BF16)
    low = (matrix - high.astype(np.float64)).astype(np.float32).astype(BF16)
    return np.stack([high, low])


def as_real(matrix):
    return np.block([[matrix.real, matrix.imag], [-matrix.imag, matrix.real]])


@functools.cache
def tables():
    j = np.arange(J)
    k1 = np.arange(HALF)
    weight = np.where((k1 == 0) | (k1 == RADIX // 2), 1.0, 2.0)[:, None]
    forward = np.exp(-2j * np.pi * np.outer(j, j) / J)
    inverse = np.exp(2j * np.pi * np.outer(j, j) / J) / TOTAL
    turn = np.exp(-2j * np.pi * np.outer(k1, j) / TOTAL)
    back = weight * turn.conj()
    matrices = np.stack(
        [split(as_real(m)) for m in (forward, inverse, inverse[:, ::-1])]
    )
    turns = np.stack([np.stack([t.real, t.imag], 1) for t in (turn, back, back[:, ::-1])])
    return matrices, turns.reshape(3 * HALF * 2, J).astype(np.float32)


def turn_rows(turn_ref, which, k):
    at = (which * HALF + k) * 2
    return (
        jnp.broadcast_to(turn_ref[at : at + 1, :], (8, J)),
        jnp.broadcast_to(turn_ref[at + 1 : at + 2, :], (8, J)),
    )


def store_spectrum(turn_ref, blocks, ref, rows):
    for k, (re, im) in enumerate(real_fft(list(blocks) + [None] * (RADIX - BLOCKS))):
        if k == 0:
            im = jnp.zeros_like(re)
        else:
            c, s = turn_rows(turn_ref, 0, k)
            if im is None:
                re, im = re * c, re * s
            else:
                re, im = re * c - im * s, re * s + im * c
        ref[k, rows, 0:J] = re
        ref[k, rows, J : 2 * J] = im


def load_blocks(turn_ref, which, ref, rows):
    spectrum = []
    for k in range(HALF):
        re, im = ref[k, rows, 0:J], ref[k, rows, J : 2 * J]
        if k == 0:
            spectrum.append((re, None))
            continue
        c, s = turn_rows(turn_ref, which, k)
        if k == RADIX // 2:
            spectrum.append((re * c - im * s, None))
        else:
            spectrum.append((re * c - im * s, re * s + im * c))
    return real_sum(spectrum)


def product(a, mat_ref, which):
    shape = a.shape
    a = a.reshape(shape[0] * shape[1], 2 * J)
    high = a.astype(BF16)
    low = (a - high.astype(F32)).astype(BF16)
    dot = functools.partial(jnp.dot, preferred_element_type=F32)
    out = dot(high, mat_ref[which, 0]) + dot(low, mat_ref[which, 0]) + dot(high, mat_ref[which, 1])
    return out.reshape(shape)


def first_part(tile, a_ref, turn_ref):
    values = [tile(p).astype(F32) for p in range(BLOCKS)]
    for half in range(2):
        rows = slice(8 * half, 8 * half + 8)
        store_spectrum(turn_ref, [v[rows] for v in values], a_ref, rows)


def transform(tiles, a_ref, outs, mat_ref, turn_ref):
    for i, tile in enumerate(tiles):
        first_part(tile, a_ref.at[pl.ds(i * HALF, HALF)], turn_ref)
    result = product(a_ref[0 : len(tiles) * HALF], mat_ref, 0)
    for i, out in enumerate(outs):
        out[...] = result[i * HALF : (i + 1) * HALF]


def both(ref, k, row):
    return (
        jnp.broadcast_to(ref[k, row : row + 1, 0:J], (8, J)),
        jnp.broadcast_to(ref[k, row : row + 1, J : 2 * J], (8, J)),
    )


def forward_terms(refl, plus, u_ref):
    def step(k, carry):
        f = [(plus[k, 8 * s : 8 * s + 8, 0:J], plus[k, 8 * s : 8 * s + 8, J : 2 * J]) for s in range(2)]
        for r in range(RCV):
            rows = slice(8 * r, 8 * r + 8)
            re, im = u_ref[k, rows, 0:J], u_ref[k, rows, J : 2 * J]
            for s in range(2):
                rr, ri = both(refl, k, 2 * r + s)
                fr, fi = f[s]
                re, im = re + (rr * fr - ri * fi), im + (rr * fi + ri * fr)
            u_ref[k, rows, 0:J] = re
            u_ref[k, rows, J : 2 * J] = im
        return carry

    lax.fori_loop(0, HALF, step, 0, unroll=True)


def backward_terms(refl, m_ref, c_ref):
    def step(k, carry):
        acc = [None, None]
        for r in range(RCV):
            rows = slice(8 * r, 8 * r + 8)
            mr, mi = m_ref[k, rows, 0:J], m_ref[k, rows, J : 2 * J]
            for s in range(2):
                rr, ri = both(refl, k, 2 * r + s)
                term = (rr * mr + ri * mi, rr * mi - ri * mr)
                acc[s] = term if acc[s] is None else cadd(acc[s], term)
        for s in range(2):
            c_ref[k, 8 * s : 8 * s + 8, 0:J] = acc[s][0]
            c_ref[k, 8 * s : 8 * s + 8, J : 2 * J] = acc[s][1]
        return carry

    lax.fori_loop(0, HALF, step, 0, unroll=True)


def window(onset, sample):
    return (sample >= BLOCKS * J // 2 - onset) & (sample <= BLOCKS * J // 2 - 1 + onset)


def middle(u_ref, a_ref, onset_ref, first, turn_ref, minus_ref):
    lane = lax.broadcasted_iota(jnp.int32, (8, J), 1)

    def step(pair, carry):
        kept = []
        for half in range(2):
            at = 2 * pair + half
            rows = pl.ds(pl.multiple_of(8 * at, 8), 8)
            mine = jnp.where(lane == first + at, onset_ref[...], 0).astype(F32)
            onset = jnp.broadcast_to(jnp.sum(mine, axis=1, keepdims=True), (8, J)).astype(jnp.int32)
            blocks = []
            for p, x in enumerate(load_blocks(turn_ref, 1, u_ref, rows)):
                blocks.append(jnp.where(window(onset, lane + p * J), x, 0.0).astype(BF16).astype(F32))
            kept.append(blocks)
            store_spectrum(turn_ref, blocks, a_ref, rows)
        for p in range(BLOCKS):
            joined = jnp.concatenate([kept[0][p], kept[1][p]], axis=0).astype(BF16)
            minus_ref[p, pl.ds(pl.multiple_of(16 * pair, 16), 16), :] = joined
        return carry

    lax.fori_loop(0, RCV // 2, step, 0)


def kernel(
    refl_ref, plus_ref, onset_r_ref, mat_hbm, turn_hbm,
    minus_out, parts, own_parts,
    refl, plus, mats, turns, onset_r,
    a_ref, hr_ref, hf_ref, u_ref, b_ref, m_ref, c_ref,
    minus, corr, peer, chip_sum,
    local_sem, one_sem, refl_sem, peer_sem,
):
    my_lag, my_src = lax.axis_index("lag"), lax.axis_index("src")
    chip, core = lax.div(my_lag, 2), lax.rem(my_lag, 2)

    def remote(source, target, send, recv, where):
        pltpu.make_async_remote_copy(
            src_ref=source, dst_ref=target, send_sem=send, recv_sem=recv, device_id=where, device_id_type=MESH
        ).start()

    def wait(ref, sem):
        pltpu.make_async_copy(ref, ref, sem).wait()

    loads = [
        (mat_hbm, mats), (turn_hbm, turns),
        (onset_r_ref.at[:, pl.ds(pl.multiple_of(my_src * J, J), J)], onset_r),
    ]
    loads = [pltpu.make_async_copy(a, b, local_sem.at[i]) for i, (a, b) in enumerate(loads)]
    for load in loads:
        load.start()

    barrier = pltpu.get_barrier_semaphore()

    def lag_at(i):
        return lax.rem(my_lag + i, LAGS)

    def src_at(d):
        return lax.rem(my_src + d, SRCS)

    def greet(lag, src):
        pl.semaphore_signal(barrier, inc=1, device_id=(lag, src), device_id_type=MESH)

    def greet_group(d, carry):
        for i in range(LAGS):
            greet(lag_at(i), src_at(d))
        return carry

    for i in range(1, LAGS):
        greet(lag_at(i), my_src)
    lax.fori_loop(1, SRCS, greet_group, 0)
    pl.semaphore_wait(barrier, LAGS * SRCS - 1)

    s_f, r_f, s_f2, r_f2, s_r, s_m, r_m, s_p, s_c, r_c, s_o, r_o = [one_sem.at[i] for i in range(12)]

    own = plus.at[core, my_src, chip]

    def same_core(i):
        return lax.rem(chip + i, CHIPS) * 2 + core

    def send_plus(d, carry):
        for i in range(CHIPS):
            remote(plus_ref, own, s_f, r_f, (same_core(i), src_at(d)))
        return carry

    def send_reflection(lag, src):
        remote(refl_ref.at[src, lag], refl.at[my_src, my_lag], s_r, refl_sem.at[my_src], (lag, src))

    def send_group(d, carry):
        for i in range(LAGS):
            send_reflection(lag_at(i), src_at(d))
        return carry

    for i in range(1, CHIPS):
        remote(plus_ref, own, s_f, r_f, (same_core(i), my_src))
    pltpu.make_async_copy(plus_ref, own, r_f).start()
    lax.fori_loop(1, SRCS, send_plus, 0)
    for i in range(1, LAGS):
        send_reflection(lag_at(i), my_src)
    pltpu.make_async_copy(refl_ref.at[my_src, my_lag], refl.at[my_src, my_lag], refl_sem.at[my_src]).start()
    lax.fori_loop(1, EARLY, send_group, 0)
    half = plus.at[core]
    other = chip * 2 + 1 - core
    wait(half, r_f)
    remote(half, half, s_f2, r_f2, (other, my_src))
    lax.fori_loop(EARLY, SRCS, send_group, 0)
    for load in loads:
        load.wait()
    u_ref[...] = jnp.zeros_like(u_ref)

    def source(d):
        return lax.rem(my_src + SRCS - d, SRCS)

    def reflection_spectra(groups):
        for g in groups:
            wait(refl.at[g], refl_sem.at[g])
        tiles = [lambda p, g=g: refl[g, p] for g in groups]
        transform(tiles, a_ref, [hr_ref.at[g] for g in groups], mats, turns)

    def early(i, carry):
        reflection_spectra([source(2 * i), source(2 * i + 1)])
        return carry

    lax.fori_loop(0, AHEAD // 2, early, 0)
    wait(half, r_f2)

    def plus_spectra(i, carry):
        tiles = [lambda p, g=g: plus[p % 2, g, p // 2] for g in (2 * i, 2 * i + 1)]
        transform(tiles, a_ref, [hf_ref.at[2 * i], hf_ref.at[2 * i + 1]], mats, turns)
        return carry

    lax.fori_loop(0, SRCS // 2, plus_spectra, 0)

    def forward(d, carry):
        g = source(d)
        pl.when(d >= AHEAD)(lambda: reflection_spectra([g]))
        forward_terms(hr_ref.at[g], hf_ref.at[g], u_ref)
        return carry

    lax.fori_loop(0, SRCS, forward, 0)
    u_ref[...] = product(u_ref[...], mats, 1)
    middle(u_ref, b_ref, onset_r, RCV * my_lag, turns, minus)

    def send_minus(i):
        remote(minus.at[lag_at(i)], minus_out.at[my_lag], s_m, r_m, (lag_at(i), my_src))

    pltpu.make_async_copy(minus.at[my_lag], minus_out.at[my_lag], r_m).start()
    for i in range(1, LAGS):
        send_minus(i)
    m_ref[...] = product(b_ref[...], mats, 0)

    def send_own():
        for i in range(1, LAGS):
            lag = lag_at(i)
            remote(corr.at[my_src, lax.rem(lag, 2), lax.div(lag, 2)], own_parts.at[my_lag], s_o, r_o, (lag, my_src))

    def add_and_send(g):
        wait(peer.at[g], peer_sem.at[g])
        chip_sum[g] = (corr[g, core].astype(F32) + peer[g].astype(F32)).astype(BF16)
        for i in range(CHIPS):
            to = lax.rem(chip + i, CHIPS)
            remote(chip_sum.at[g, to], parts.at[my_src, chip], s_c, r_c, (to * 2 + core, g))

    def backward(d, carry):
        g = src_at(d)
        backward_terms(hr_ref.at[g], m_ref, c_ref)
        c_ref[...] = product(c_ref[...], mats, 2)
        kept = [load_blocks(turns, 2, c_ref, slice(8 * h, 8 * h + 8)) for h in range(2)]
        for p in range(BLOCKS):
            at = BLOCKS - 1 - p
            corr[g, p % 2, p // 2] = jnp.concatenate([kept[0][at], kept[1][at]], axis=0).astype(BF16)

        @pl.when(d < SRCS)
        def _():
            remote(corr.at[g, 1 - core], peer.at[g], s_p, peer_sem.at[g], (other, my_src))

        pl.when(d == SRCS)(send_own)
        pl.when(d > DEPTH)(lambda: add_and_send(src_at(d - DEPTH)))
        return carry

    lax.fori_loop(1, SRCS + 1, backward, 0)
    for d in range(SRCS + 1 - DEPTH, SRCS):
        add_and_send(src_at(d))
    pltpu.make_async_copy(corr.at[my_src, core, chip], own_parts.at[my_lag], r_o).start()

    wait(parts.at[pl.ds(0, SRCS - 1)], r_c)
    wait(own_parts, r_o)
    wait(minus_out, r_m)
    wait(half.at[pl.ds(0, SRCS - 1)], s_f)
    wait(half.at[0, pl.ds(0, CHIPS - 1)], s_f)
    wait(half, s_f2)
    wait(refl.at[pl.ds(0, SRCS - 1)], s_r)
    wait(refl.at[0, pl.ds(0, LAGS - 1)], s_r)
    wait(minus_out.at[pl.ds(0, LAGS - 1)], s_m)
    wait(peer.at[pl.ds(0, SRCS - 1)], s_p)
    wait(parts.at[pl.ds(0, SRCS - 1)], s_c)
    wait(own_parts.at[pl.ds(0, LAGS - 1)], s_o)


def finish_kernel(minus_ref, parts, own_parts, start, onset_s, minus_out, next_out):
    my_lag, my_src = lax.axis_index("lag"), lax.axis_index("src")
    minus_out[...] = minus_ref[...]
    lane = lax.broadcasted_iota(jnp.int32, (8, J), 1)
    sums = [own_parts[l].astype(F32) for l in range(4)]
    for l in range(4, LAGS):
        sums[l % 4] = sums[l % 4] + own_parts[l].astype(F32)
    for d in range(1, SRCS):
        g = lax.rem(my_src + d, SRCS)
        for l in range(CHIPS):
            sums[l % 4] = sums[l % 4] + parts[g, l].astype(F32)
    total = (sums[0] + sums[1]) + (sums[2] + sums[3])
    begin = start[...].astype(F32)
    for s in range(2):
        row = jnp.broadcast_to(onset_s[s : s + 1, :], (8, 8)).astype(F32)
        pick = lax.broadcasted_iota(jnp.int32, (8, 8), 0) == lax.broadcasted_iota(jnp.int32, (8, 8), 1)
        onset = jnp.sum(jnp.where(pick, row, 0.0), axis=1, keepdims=True)
        mask = window(jnp.broadcast_to(onset, (8, J)).astype(jnp.int32), lane + my_lag * J)
        rows = slice(8 * s, 8 * s + 8)
        next_out[rows, :] = begin[rows] + jnp.where(mask, total[rows], 0.0)


def body(reflection, focus_plus, focus_start, onset_receiver, onset_source):
    vmem = pl.BlockSpec(memory_space=pltpu.VMEM)
    matrices, turns = tables()
    spectra = pltpu.VMEM((SRCS, HALF, 16, 2 * J), F32)
    tiles = pltpu.VMEM((SRCS, CHIPS, 16, J), BF16)
    minus_out, parts, own_parts = pl.pallas_call(
        kernel,
        out_shape=(
            jax.ShapeDtypeStruct((LAGS, 8 * RCV, J), BF16),
            jax.ShapeDtypeStruct((SRCS, CHIPS, 16, J), BF16),
            jax.ShapeDtypeStruct((LAGS, 16, J), BF16),
        ),
        in_specs=[pl.BlockSpec(memory_space=pl.ANY)] * 5,
        out_specs=(pl.BlockSpec(memory_space=pl.ANY),) * 3,
        scratch_shapes=[
            pltpu.VMEM((SRCS, LAGS, 16, J), BF16),
            pltpu.VMEM((2, SRCS, CHIPS, 16, J), BF16),
            pltpu.VMEM(matrices.shape, BF16),
            pltpu.VMEM(turns.shape, F32),
            pltpu.VMEM((8, J), jnp.int32),
            pltpu.VMEM((2 * HALF, 16, 2 * J), F32),
            spectra,
            spectra,
            pltpu.VMEM((HALF, 64, 2 * J), F32),
            pltpu.VMEM((HALF, 64, 2 * J), F32),
            pltpu.VMEM((HALF, 64, 2 * J), F32),
            pltpu.VMEM((HALF, 16, 2 * J), F32),
            pltpu.VMEM((LAGS, 8 * RCV, J), BF16),
            pltpu.VMEM((SRCS, 2, CHIPS, 16, J), BF16),
            tiles,
            tiles,
            pltpu.SemaphoreType.DMA((3,)),
            pltpu.SemaphoreType.DMA((12,)),
            pltpu.SemaphoreType.DMA((SRCS,)),
            pltpu.SemaphoreType.DMA((SRCS,)),
        ],
        compiler_params=pltpu.CompilerParams(
            collective_id=0, has_side_effects=True, vmem_limit_bytes=60 * 2**20
        ),
        name="focus",
    )(
        reflection.reshape(SRCS, LAGS, 16, J),
        focus_plus.reshape(16, J),
        onset_receiver.T,
        jnp.asarray(matrices),
        jnp.asarray(turns),
    )
    minus_out, next_out = pl.pallas_call(
        finish_kernel,
        out_shape=(
            jax.ShapeDtypeStruct(minus_out.shape, BF16),
            jax.ShapeDtypeStruct((16, J), F32),
        ),
        in_specs=[vmem] * 5,
        out_specs=(vmem, vmem),
        name="finish",
    )(minus_out, parts, own_parts, focus_start.reshape(16, J), onset_source)
    return minus_out.reshape(J, 8, J), next_out.reshape(2, 8, J)


def solution(mesh):
    return jax.shard_map(
        body,
        mesh=mesh,
        in_specs=(
            P(None, "src", "lag"),
            P("src", None, "lag"),
            P("src", None, "lag"),
            P(),
            P("src", None),
        ),
        out_specs=(P("src", None, "lag"), P("src", None, "lag")),
        check_vma=False,
    )
```

```python
import functools
import math

import jax
import jax.numpy as jnp
import numpy as np
from jax import lax
from jax.experimental import pallas as pl
from jax.experimental.pallas import tpu as pltpu
from jax.sharding import PartitionSpec as P

MESH = pl.DeviceIdType.MESH
LAGS, SRCS = 16, 8
CHIPS = LAGS // 2
RCV = 8
EARLY = 7
AHEAD = 2
J = 128
BLOCKS = 16
RADIX = 32
HALF = RADIX // 2 + 1
TOTAL = RADIX * J
F32, BF16 = jnp.float32, jnp.bfloat16


def add(a, b):
    if a is None or b is None:
        return b if a is None else a
    return a + b


def sub(a, b):
    if b is None:
        return a
    return -b if a is None else a - b


def neg(a):
    return None if a is None else -a


def scale(a, c):
    if a is None or c == 0.0:
        return None
    if c == 1.0:
        return a
    return -a if c == -1.0 else a * c


def root(n, k, sign):
    k = k % n
    if 4 * k % n == 0:
        c, s = [(1.0, 0.0), (0.0, 1.0), (-1.0, 0.0), (0.0, -1.0)][4 * k // n]
    else:
        c, s = math.cos(2 * math.pi * k / n), math.sin(2 * math.pi * k / n)
    return c, sign * s


def times(z, w):
    (re, im), (c, s) = z, w
    if re is not None and im is not None and abs(abs(c) - abs(s)) < 1e-12:
        h = abs(c)
        a, b = math.copysign(1.0, c), math.copysign(1.0, s)
        first = re if a > 0 else -re
        second = re if b > 0 else -re
        return (
            (first - im if b > 0 else first + im) * h,
            (second + im if a > 0 else second - im) * h,
        )
    return sub(scale(re, c), scale(im, s)), add(scale(re, s), scale(im, c))


def cadd(a, b):
    return add(a[0], b[0]), add(a[1], b[1])


def csub(a, b):
    return sub(a[0], b[0]), sub(a[1], b[1])


def cfft(values, sign):
    n = len(values)
    if n == 1:
        return values
    even, odd = cfft(values[0::2], sign), cfft(values[1::2], sign)
    odd = [times(v, root(n, k, sign)) for k, v in enumerate(odd)]
    return [cadd(a, b) for a, b in zip(even, odd)] + [csub(a, b) for a, b in zip(even, odd)]


def real_fft(x):
    n = len(x)
    if n == 1:
        return [(x[0], None)]
    half = n // 2
    z = [add(x[p], x[p + half]) for p in range(half)]
    d = [sub(x[p], x[p + half]) for p in range(half)]
    out = [None] * (half + 1)
    if n == 2:
        return [(z[0], None), (d[0], None)]
    out[0::2] = real_fft(z)
    quarter = n // 4
    turned = [times((d[p], neg(d[p + quarter])), root(n, p, -1)) for p in range(quarter)]
    for q, v in enumerate(cfft(turned, -1)):
        k = 4 * q + 1
        if k <= half:
            out[k] = v
        else:
            out[n - k] = (v[0], neg(v[1]))
    return out


def real_sum(spectrum):
    n = 2 * (len(spectrum) - 1)
    half = n // 2
    if n == 2:
        return [spectrum[0][0] + spectrum[1][0], spectrum[0][0] - spectrum[1][0]]
    even = real_sum(spectrum[0::2])
    quarter = n // 4
    terms = []
    for q in range(quarter):
        k = 4 * q + 1
        terms.append(spectrum[k] if k <= half else (spectrum[n - k][0], -spectrum[n - k][1]))
    turned = [times(v, root(n, p, 1)) for p, v in enumerate(cfft(terms, 1))]
    odd = [v[0] for v in turned] + [-v[1] for v in turned]
    if n == RADIX:
        return [even[p] + odd[p] for p in range(half)]
    return [even[p] + odd[p] for p in range(half)] + [even[p] - odd[p] for p in range(half)]


def split(matrix):
    high = matrix.astype(np.float32).astype(BF16)
    low = (matrix - high.astype(np.float64)).astype(np.float32).astype(BF16)
    return np.stack([high, low])


def as_real(matrix):
    return np.block([[matrix.real, matrix.imag], [-matrix.imag, matrix.real]])


@functools.cache
def tables():
    j = np.arange(J)
    k1 = np.arange(HALF)
    weight = np.where((k1 == 0) | (k1 == RADIX // 2), 1.0, 2.0)[:, None]
    forward = np.exp(-2j * np.pi * np.outer(j, j) / J)
    inverse = np.exp(2j * np.pi * np.outer(j, j) / J) / TOTAL
    turn = np.exp(-2j * np.pi * np.outer(k1, j) / TOTAL)
    back = weight * turn.conj()
    matrices = np.stack(
        [split(as_real(m)) for m in (forward, inverse, inverse[:, ::-1])]
    )
    turns = np.stack([np.stack([t.real, t.imag], 1) for t in (turn, back, back[:, ::-1])])
    return matrices, turns.reshape(3 * HALF * 2, J).astype(np.float32)


def turn_rows(turn_ref, which, k):
    at = (which * HALF + k) * 2
    return (
        jnp.broadcast_to(turn_ref[at : at + 1, :], (8, J)),
        jnp.broadcast_to(turn_ref[at + 1 : at + 2, :], (8, J)),
    )


def store_spectrum(turn_ref, blocks, ref, rows):
    for k, (re, im) in enumerate(real_fft(list(blocks) + [None] * (RADIX - BLOCKS))):
        if k == 0:
            im = jnp.zeros_like(re)
        else:
            c, s = turn_rows(turn_ref, 0, k)
            if im is None:
                re, im = re * c, re * s
            else:
                re, im = re * c - im * s, re * s + im * c
        ref[k, rows, 0:J] = re
        ref[k, rows, J : 2 * J] = im


def load_blocks(turn_ref, which, ref, rows):
    spectrum = []
    for k in range(HALF):
        re, im = ref[k, rows, 0:J], ref[k, rows, J : 2 * J]
        if k == 0:
            spectrum.append((re, None))
            continue
        c, s = turn_rows(turn_ref, which, k)
        if k == RADIX // 2:
            spectrum.append((re * c - im * s, None))
        else:
            spectrum.append((re * c - im * s, re * s + im * c))
    return real_sum(spectrum)


def product(a, mat_ref, which):
    shape = a.shape
    a = a.reshape(shape[0] * shape[1], 2 * J)
    high = a.astype(BF16)
    low = (a - high.astype(F32)).astype(BF16)
    dot = functools.partial(jnp.dot, preferred_element_type=F32)
    out = dot(high, mat_ref[which, 0]) + dot(low, mat_ref[which, 0]) + dot(high, mat_ref[which, 1])
    return out.reshape(shape)


def first_part(tile, a_ref, turn_ref):
    values = [tile(p).astype(F32) for p in range(BLOCKS)]
    for half in range(2):
        rows = slice(8 * half, 8 * half + 8)
        store_spectrum(turn_ref, [v[rows] for v in values], a_ref, rows)


def transform(tiles, a_ref, outs, mat_ref, turn_ref):
    for i, tile in enumerate(tiles):
        first_part(tile, a_ref.at[pl.ds(i * HALF, HALF)], turn_ref)
    result = product(a_ref[0 : len(tiles) * HALF], mat_ref, 0)
    for i, out in enumerate(outs):
        out[...] = result[i * HALF : (i + 1) * HALF]


def both(ref, k, row):
    return (
        jnp.broadcast_to(ref[k, row : row + 1, 0:J], (8, J)),
        jnp.broadcast_to(ref[k, row : row + 1, J : 2 * J], (8, J)),
    )


def forward_terms(refl, plus, u_ref):
    def step(k, carry):
        f = [(plus[k, 8 * s : 8 * s + 8, 0:J], plus[k, 8 * s : 8 * s + 8, J : 2 * J]) for s in range(2)]
        for r in range(RCV):
            rows = slice(8 * r, 8 * r + 8)
            re, im = u_ref[k, rows, 0:J], u_ref[k, rows, J : 2 * J]
            for s in range(2):
                rr, ri = both(refl, k, 2 * r + s)
                fr, fi = f[s]
                re, im = re + (rr * fr - ri * fi), im + (rr * fi + ri * fr)
            u_ref[k, rows, 0:J] = re
            u_ref[k, rows, J : 2 * J] = im
        return carry

    lax.fori_loop(0, HALF, step, 0, unroll=True)


def backward_terms(refl, m_ref, c_ref):
    def step(k, carry):
        acc = [None, None]
        for r in range(RCV):
            rows = slice(8 * r, 8 * r + 8)
            mr, mi = m_ref[k, rows, 0:J], m_ref[k, rows, J : 2 * J]
            for s in range(2):
                rr, ri = both(refl, k, 2 * r + s)
                term = (rr * mr + ri * mi, rr * mi - ri * mr)
                acc[s] = term if acc[s] is None else cadd(acc[s], term)
        for s in range(2):
            c_ref[k, 8 * s : 8 * s + 8, 0:J] = acc[s][0]
            c_ref[k, 8 * s : 8 * s + 8, J : 2 * J] = acc[s][1]
        return carry

    lax.fori_loop(0, HALF, step, 0, unroll=True)


def window(onset, sample):
    return (sample >= BLOCKS * J // 2 - onset) & (sample <= BLOCKS * J // 2 - 1 + onset)


def middle(u_ref, a_ref, onset_ref, first, turn_ref, minus_ref):
    lane = lax.broadcasted_iota(jnp.int32, (8, J), 1)

    def step(pair, carry):
        kept = []
        for half in range(2):
            at = 2 * pair + half
            rows = pl.ds(pl.multiple_of(8 * at, 8), 8)
            mine = jnp.where(lane == first + at, onset_ref[...], 0).astype(F32)
            onset = jnp.broadcast_to(jnp.sum(mine, axis=1, keepdims=True), (8, J)).astype(jnp.int32)
            blocks = []
            for p, x in enumerate(load_blocks(turn_ref, 1, u_ref, rows)):
                blocks.append(jnp.where(window(onset, lane + p * J), x, 0.0).astype(BF16).astype(F32))
            kept.append(blocks)
            store_spectrum(turn_ref, blocks, a_ref, rows)
        for p in range(BLOCKS):
            joined = jnp.concatenate([kept[0][p], kept[1][p]], axis=0).astype(BF16)
            minus_ref[p, pl.ds(pl.multiple_of(16 * pair, 16), 16), :] = joined
        return carry

    lax.fori_loop(0, RCV // 2, step, 0)


def kernel(
    refl_ref, plus_ref, onset_r_ref, mat_hbm, turn_hbm,
    minus_out, parts, own_parts,
    refl, plus, mats, turns, onset_r,
    a_ref, hr_ref, hf_ref, u_ref, b_ref, m_ref, c_ref,
    minus, corr, peer, chip_sum,
    local_sem, one_sem, refl_sem, peer_sem,
):
    my_lag, my_src = lax.axis_index("lag"), lax.axis_index("src")
    chip, core = lax.div(my_lag, 2), lax.rem(my_lag, 2)

    def remote(source, target, send, recv, where):
        pltpu.make_async_remote_copy(
            src_ref=source, dst_ref=target, send_sem=send, recv_sem=recv, device_id=where, device_id_type=MESH
        ).start()

    def wait(ref, sem):
        pltpu.make_async_copy(ref, ref, sem).wait()

    loads = [
        (mat_hbm, mats), (turn_hbm, turns),
        (onset_r_ref.at[:, pl.ds(pl.multiple_of(my_src * J, J), J)], onset_r),
    ]
    loads = [pltpu.make_async_copy(a, b, local_sem.at[i]) for i, (a, b) in enumerate(loads)]
    for load in loads:
        load.start()

    barrier = pltpu.get_barrier_semaphore()

    def lag_at(i):
        return lax.rem(my_lag + i, LAGS)

    def src_at(d):
        return lax.rem(my_src + d, SRCS)

    def greet(lag, src):
        pl.semaphore_signal(barrier, inc=1, device_id=(lag, src), device_id_type=MESH)

    def greet_group(d, carry):
        for i in range(LAGS):
            greet(lag_at(i), src_at(d))
        return carry

    for i in range(1, LAGS):
        greet(lag_at(i), my_src)
    lax.fori_loop(1, SRCS, greet_group, 0)
    pl.semaphore_wait(barrier, LAGS * SRCS - 1)

    s_f, r_f, s_f2, r_f2, s_r, s_m, r_m, s_p, s_c, r_c, s_o, r_o = [one_sem.at[i] for i in range(12)]

    own = plus.at[core, my_src, chip]

    def same_core(i):
        return lax.rem(chip + i, CHIPS) * 2 + core

    def send_plus(d, carry):
        for i in range(CHIPS):
            remote(plus_ref, own, s_f, r_f, (same_core(i), src_at(d)))
        return carry

    def send_reflection(lag, src):
        remote(refl_ref.at[src, lag], refl.at[my_src, my_lag], s_r, refl_sem.at[my_src], (lag, src))

    def send_group(d, carry):
        for i in range(LAGS):
            send_reflection(lag_at(i), src_at(d))
        return carry

    for i in range(1, CHIPS):
        remote(plus_ref, own, s_f, r_f, (same_core(i), my_src))
    pltpu.make_async_copy(plus_ref, own, r_f).start()
    lax.fori_loop(1, SRCS, send_plus, 0)
    for i in range(1, LAGS):
        send_reflection(lag_at(i), my_src)
    pltpu.make_async_copy(refl_ref.at[my_src, my_lag], refl.at[my_src, my_lag], refl_sem.at[my_src]).start()
    lax.fori_loop(1, EARLY, send_group, 0)
    half = plus.at[core]
    other = chip * 2 + 1 - core
    wait(half, r_f)
    remote(half, half, s_f2, r_f2, (other, my_src))
    lax.fori_loop(EARLY, SRCS, send_group, 0)
    for load in loads:
        load.wait()
    u_ref[...] = jnp.zeros_like(u_ref)

    def source(d):
        return lax.rem(my_src + SRCS - d, SRCS)

    def reflection_spectra(groups):
        for g in groups:
            wait(refl.at[g], refl_sem.at[g])
        tiles = [lambda p, g=g: refl[g, p] for g in groups]
        transform(tiles, a_ref, [hr_ref.at[g] for g in groups], mats, turns)

    def early(i, carry):
        reflection_spectra([source(2 * i), source(2 * i + 1)])
        return carry

    lax.fori_loop(0, AHEAD // 2, early, 0)
    wait(half, r_f2)

    def plus_spectra(i, carry):
        tiles = [lambda p, g=g: plus[p % 2, g, p // 2] for g in (2 * i, 2 * i + 1)]
        transform(tiles, a_ref, [hf_ref.at[2 * i], hf_ref.at[2 * i + 1]], mats, turns)
        return carry

    lax.fori_loop(0, SRCS // 2, plus_spectra, 0)

    def forward(d, carry):
        g = source(d)
        pl.when(d >= AHEAD)(lambda: reflection_spectra([g]))
        forward_terms(hr_ref.at[g], hf_ref.at[g], u_ref)
        return carry

    lax.fori_loop(0, SRCS, forward, 0)
    u_ref[...] = product(u_ref[...], mats, 1)
    middle(u_ref, b_ref, onset_r, RCV * my_lag, turns, minus)

    def send_minus(i):
        remote(minus.at[lag_at(i)], minus_out.at[my_lag], s_m, r_m, (lag_at(i), my_src))

    pltpu.make_async_copy(minus.at[my_lag], minus_out.at[my_lag], r_m).start()
    for i in range(1, LAGS):
        send_minus(i)
    m_ref[...] = product(b_ref[...], mats, 0)

    def send_own():
        for i in range(1, LAGS):
            lag = lag_at(i)
            remote(corr.at[my_src, lax.rem(lag, 2), lax.div(lag, 2)], own_parts.at[my_lag], s_o, r_o, (lag, my_src))

    def add_and_send(g):
        wait(peer.at[g], peer_sem.at[g])
        chip_sum[g] = (corr[g, core].astype(F32) + peer[g].astype(F32)).astype(BF16)
        for i in range(CHIPS):
            to = lax.rem(chip + i, CHIPS)
            remote(chip_sum.at[g, to], parts.at[my_src, chip], s_c, r_c, (to * 2 + core, g))

    def partial_sums(groups):
        for h, g in enumerate(groups):
            backward_terms(hr_ref.at[g], m_ref, c_ref.at[pl.ds(h * HALF, HALF)])
        filled = slice(0, len(groups) * HALF)
        c_ref[filled] = product(c_ref[filled], mats, 2)
        for h, g in enumerate(groups):
            c_part = c_ref.at[pl.ds(h * HALF, HALF)]
            kept = [load_blocks(turns, 2, c_part, slice(8 * s, 8 * s + 8)) for s in range(2)]
            for p in range(BLOCKS):
                at = BLOCKS - 1 - p
                corr[g, p % 2, p // 2] = jnp.concatenate([kept[0][at], kept[1][at]], axis=0).astype(BF16)

    def to_other_core(g):
        remote(corr.at[g, 1 - core], peer.at[g], s_p, peer_sem.at[g], (other, my_src))

    def backward(i, carry):
        groups = [src_at(2 * i + 1), src_at(2 * i + 2)]
        partial_sums(groups)
        for g in groups:
            to_other_core(g)

        @pl.when(i > 0)
        def _():
            add_and_send(src_at(2 * i - 1))
            add_and_send(src_at(2 * i))

        return carry

    lax.fori_loop(0, SRCS // 2 - 1, backward, 0)
    partial_sums([src_at(SRCS - 1)])
    to_other_core(src_at(SRCS - 1))
    add_and_send(src_at(SRCS - 3))
    add_and_send(src_at(SRCS - 2))
    partial_sums([my_src])
    send_own()
    add_and_send(src_at(SRCS - 1))
    pltpu.make_async_copy(corr.at[my_src, core, chip], own_parts.at[my_lag], r_o).start()

    wait(parts.at[pl.ds(0, SRCS - 1)], r_c)
    wait(own_parts, r_o)
    wait(minus_out, r_m)
    wait(half.at[pl.ds(0, SRCS - 1)], s_f)
    wait(half.at[0, pl.ds(0, CHIPS - 1)], s_f)
    wait(half, s_f2)
    wait(refl.at[pl.ds(0, SRCS - 1)], s_r)
    wait(refl.at[0, pl.ds(0, LAGS - 1)], s_r)
    wait(minus_out.at[pl.ds(0, LAGS - 1)], s_m)
    wait(peer.at[pl.ds(0, SRCS - 1)], s_p)
    wait(parts.at[pl.ds(0, SRCS - 1)], s_c)
    wait(own_parts.at[pl.ds(0, LAGS - 1)], s_o)


def finish_kernel(minus_ref, parts, own_parts, start, onset_s, minus_out, next_out):
    my_lag, my_src = lax.axis_index("lag"), lax.axis_index("src")
    minus_out[...] = minus_ref[...]
    lane = lax.broadcasted_iota(jnp.int32, (8, J), 1)
    sums = [own_parts[l].astype(F32) for l in range(4)]
    for l in range(4, LAGS):
        sums[l % 4] = sums[l % 4] + own_parts[l].astype(F32)
    for d in range(1, SRCS):
        g = lax.rem(my_src + d, SRCS)
        for l in range(CHIPS):
            sums[l % 4] = sums[l % 4] + parts[g, l].astype(F32)
    total = (sums[0] + sums[1]) + (sums[2] + sums[3])
    begin = start[...].astype(F32)
    for s in range(2):
        row = jnp.broadcast_to(onset_s[s : s + 1, :], (8, 8)).astype(F32)
        pick = lax.broadcasted_iota(jnp.int32, (8, 8), 0) == lax.broadcasted_iota(jnp.int32, (8, 8), 1)
        onset = jnp.sum(jnp.where(pick, row, 0.0), axis=1, keepdims=True)
        mask = window(jnp.broadcast_to(onset, (8, J)).astype(jnp.int32), lane + my_lag * J)
        rows = slice(8 * s, 8 * s + 8)
        next_out[rows, :] = begin[rows] + jnp.where(mask, total[rows], 0.0)


def body(reflection, focus_plus, focus_start, onset_receiver, onset_source):
    vmem = pl.BlockSpec(memory_space=pltpu.VMEM)
    matrices, turns = tables()
    spectra = pltpu.VMEM((SRCS, HALF, 16, 2 * J), F32)
    tiles = pltpu.VMEM((SRCS, CHIPS, 16, J), BF16)
    minus_out, parts, own_parts = pl.pallas_call(
        kernel,
        out_shape=(
            jax.ShapeDtypeStruct((LAGS, 8 * RCV, J), BF16),
            jax.ShapeDtypeStruct((SRCS, CHIPS, 16, J), BF16),
            jax.ShapeDtypeStruct((LAGS, 16, J), BF16),
        ),
        in_specs=[pl.BlockSpec(memory_space=pl.ANY)] * 5,
        out_specs=(pl.BlockSpec(memory_space=pl.ANY),) * 3,
        scratch_shapes=[
            pltpu.VMEM((SRCS, LAGS, 16, J), BF16),
            pltpu.VMEM((2, SRCS, CHIPS, 16, J), BF16),
            pltpu.VMEM(matrices.shape, BF16),
            pltpu.VMEM(turns.shape, F32),
            pltpu.VMEM((8, J), jnp.int32),
            pltpu.VMEM((2 * HALF, 16, 2 * J), F32),
            spectra,
            spectra,
            pltpu.VMEM((HALF, 64, 2 * J), F32),
            pltpu.VMEM((HALF, 64, 2 * J), F32),
            pltpu.VMEM((HALF, 64, 2 * J), F32),
            pltpu.VMEM((2 * HALF, 16, 2 * J), F32),
            pltpu.VMEM((LAGS, 8 * RCV, J), BF16),
            pltpu.VMEM((SRCS, 2, CHIPS, 16, J), BF16),
            tiles,
            tiles,
            pltpu.SemaphoreType.DMA((3,)),
            pltpu.SemaphoreType.DMA((12,)),
            pltpu.SemaphoreType.DMA((SRCS,)),
            pltpu.SemaphoreType.DMA((SRCS,)),
        ],
        compiler_params=pltpu.CompilerParams(
            collective_id=0, has_side_effects=True, vmem_limit_bytes=60 * 2**20
        ),
        name="focus",
    )(
        reflection.reshape(SRCS, LAGS, 16, J),
        focus_plus.reshape(16, J),
        onset_receiver.T,
        jnp.asarray(matrices),
        jnp.asarray(turns),
    )
    minus_out, next_out = pl.pallas_call(
        finish_kernel,
        out_shape=(
            jax.ShapeDtypeStruct(minus_out.shape, BF16),
            jax.ShapeDtypeStruct((16, J), F32),
        ),
        in_specs=[vmem] * 5,
        out_specs=(vmem, vmem),
        name="finish",
    )(minus_out, parts, own_parts, focus_start.reshape(16, J), onset_source)
    return minus_out.reshape(J, 8, J), next_out.reshape(2, 8, J)


def solution(mesh):
    return jax.shard_map(
        body,
        mesh=mesh,
        in_specs=(
            P(None, "src", "lag"),
            P("src", None, "lag"),
            P("src", None, "lag"),
            P(),
            P("src", None),
        ),
        out_specs=(P("src", None, "lag"), P("src", None, "lag")),
        check_vma=False,
    )
```

```python
import functools
import math

import jax
import jax.numpy as jnp
import numpy as np
from jax import lax
from jax.experimental import pallas as pl
from jax.experimental.pallas import tpu as pltpu
from jax.sharding import PartitionSpec as P

MESH = pl.DeviceIdType.MESH
LAGS, SRCS = 16, 8
CHIPS = LAGS // 2
RCV = 8
EARLY = 8
AHEAD = 2
J = 128
BLOCKS = 16
RADIX = 32
HALF = RADIX // 2 + 1
TOTAL = RADIX * J
F32, BF16 = jnp.float32, jnp.bfloat16


def add(a, b):
    if a is None or b is None:
        return b if a is None else a
    return a + b


def sub(a, b):
    if b is None:
        return a
    return -b if a is None else a - b


def neg(a):
    return None if a is None else -a


def scale(a, c):
    if a is None or c == 0.0:
        return None
    if c == 1.0:
        return a
    return -a if c == -1.0 else a * c


def root(n, k, sign):
    k = k % n
    if 4 * k % n == 0:
        c, s = [(1.0, 0.0), (0.0, 1.0), (-1.0, 0.0), (0.0, -1.0)][4 * k // n]
    else:
        c, s = math.cos(2 * math.pi * k / n), math.sin(2 * math.pi * k / n)
    return c, sign * s


def times(z, w):
    (re, im), (c, s) = z, w
    if re is not None and im is not None and abs(abs(c) - abs(s)) < 1e-12:
        h = abs(c)
        a, b = math.copysign(1.0, c), math.copysign(1.0, s)
        first = re if a > 0 else -re
        second = re if b > 0 else -re
        return (
            (first - im if b > 0 else first + im) * h,
            (second + im if a > 0 else second - im) * h,
        )
    return sub(scale(re, c), scale(im, s)), add(scale(re, s), scale(im, c))


def cadd(a, b):
    return add(a[0], b[0]), add(a[1], b[1])


def csub(a, b):
    return sub(a[0], b[0]), sub(a[1], b[1])


def cfft(values, sign):
    n = len(values)
    if n == 1:
        return values
    even, odd = cfft(values[0::2], sign), cfft(values[1::2], sign)
    odd = [times(v, root(n, k, sign)) for k, v in enumerate(odd)]
    return [cadd(a, b) for a, b in zip(even, odd)] + [csub(a, b) for a, b in zip(even, odd)]


def real_fft(x):
    n = len(x)
    if n == 1:
        return [(x[0], None)]
    half = n // 2
    z = [add(x[p], x[p + half]) for p in range(half)]
    d = [sub(x[p], x[p + half]) for p in range(half)]
    out = [None] * (half + 1)
    if n == 2:
        return [(z[0], None), (d[0], None)]
    out[0::2] = real_fft(z)
    quarter = n // 4
    turned = [times((d[p], neg(d[p + quarter])), root(n, p, -1)) for p in range(quarter)]
    for q, v in enumerate(cfft(turned, -1)):
        k = 4 * q + 1
        if k <= half:
            out[k] = v
        else:
            out[n - k] = (v[0], neg(v[1]))
    return out


def real_sum(spectrum):
    n = 2 * (len(spectrum) - 1)
    half = n // 2
    if n == 2:
        return [spectrum[0][0] + spectrum[1][0], spectrum[0][0] - spectrum[1][0]]
    even = real_sum(spectrum[0::2])
    quarter = n // 4
    terms = []
    for q in range(quarter):
        k = 4 * q + 1
        terms.append(spectrum[k] if k <= half else (spectrum[n - k][0], -spectrum[n - k][1]))
    turned = [times(v, root(n, p, 1)) for p, v in enumerate(cfft(terms, 1))]
    odd = [v[0] for v in turned] + [-v[1] for v in turned]
    if n == RADIX:
        return [even[p] + odd[p] for p in range(half)]
    return [even[p] + odd[p] for p in range(half)] + [even[p] - odd[p] for p in range(half)]


def split(matrix):
    high = matrix.astype(np.float32).astype(BF16)
    low = (matrix - high.astype(np.float64)).astype(np.float32).astype(BF16)
    return np.stack([high, low])


def as_real(matrix):
    return np.block([[matrix.real, matrix.imag], [-matrix.imag, matrix.real]])


@functools.cache
def tables():
    j = np.arange(J)
    k1 = np.arange(HALF)
    weight = np.where((k1 == 0) | (k1 == RADIX // 2), 1.0, 2.0)[:, None]
    forward = np.exp(-2j * np.pi * np.outer(j, j) / J)
    inverse = np.exp(2j * np.pi * np.outer(j, j) / J) / TOTAL
    turn = np.exp(-2j * np.pi * np.outer(k1, j) / TOTAL)
    back = weight * turn.conj()
    matrices = np.stack(
        [split(as_real(m)) for m in (forward, inverse, inverse[:, ::-1])]
    )
    turns = np.stack([np.stack([t.real, t.imag], 1) for t in (turn, back, back[:, ::-1])])
    return matrices, turns.reshape(3 * HALF * 2, J).astype(np.float32)


def turn_rows(turn_ref, which, k):
    at = (which * HALF + k) * 2
    return (
        jnp.broadcast_to(turn_ref[at : at + 1, :], (8, J)),
        jnp.broadcast_to(turn_ref[at + 1 : at + 2, :], (8, J)),
    )


def store_spectrum(turn_ref, blocks, ref, rows):
    for k, (re, im) in enumerate(real_fft(list(blocks) + [None] * (RADIX - BLOCKS))):
        if k == 0:
            im = jnp.zeros_like(re)
        else:
            c, s = turn_rows(turn_ref, 0, k)
            if im is None:
                re, im = re * c, re * s
            else:
                re, im = re * c - im * s, re * s + im * c
        ref[k, rows, 0:J] = re
        ref[k, rows, J : 2 * J] = im


def load_blocks(turn_ref, which, ref, rows):
    spectrum = []
    for k in range(HALF):
        re, im = ref[k, rows, 0:J], ref[k, rows, J : 2 * J]
        if k == 0:
            spectrum.append((re, None))
            continue
        c, s = turn_rows(turn_ref, which, k)
        if k == RADIX // 2:
            spectrum.append((re * c - im * s, None))
        else:
            spectrum.append((re * c - im * s, re * s + im * c))
    return real_sum(spectrum)


def product(a, mat_ref, which):
    shape = a.shape
    a = a.reshape(shape[0] * shape[1], 2 * J)
    high = a.astype(BF16)
    low = (a - high.astype(F32)).astype(BF16)
    dot = functools.partial(jnp.dot, preferred_element_type=F32)
    out = dot(high, mat_ref[which, 0]) + dot(low, mat_ref[which, 0]) + dot(high, mat_ref[which, 1])
    return out.reshape(shape)


def first_part(tile, a_ref, turn_ref):
    values = [tile(p).astype(F32) for p in range(BLOCKS)]
    for half in range(2):
        rows = slice(8 * half, 8 * half + 8)
        store_spectrum(turn_ref, [v[rows] for v in values], a_ref, rows)


def transform(tiles, a_ref, outs, mat_ref, turn_ref):
    for i, tile in enumerate(tiles):
        first_part(tile, a_ref.at[pl.ds(i * HALF, HALF)], turn_ref)
    result = product(a_ref[0 : len(tiles) * HALF], mat_ref, 0)
    for i, out in enumerate(outs):
        out[...] = result[i * HALF : (i + 1) * HALF]


def both(ref, k, row):
    return (
        jnp.broadcast_to(ref[k, row : row + 1, 0:J], (8, J)),
        jnp.broadcast_to(ref[k, row : row + 1, J : 2 * J], (8, J)),
    )


def forward_terms(refl, plus, u_ref):
    def step(k, carry):
        f = [(plus[k, 8 * s : 8 * s + 8, 0:J], plus[k, 8 * s : 8 * s + 8, J : 2 * J]) for s in range(2)]
        for r in range(RCV):
            rows = slice(8 * r, 8 * r + 8)
            re, im = u_ref[k, rows, 0:J], u_ref[k, rows, J : 2 * J]
            for s in range(2):
                rr, ri = both(refl, k, 2 * r + s)
                fr, fi = f[s]
                re, im = re + (rr * fr - ri * fi), im + (rr * fi + ri * fr)
            u_ref[k, rows, 0:J] = re
            u_ref[k, rows, J : 2 * J] = im
        return carry

    lax.fori_loop(0, HALF, step, 0, unroll=True)


def backward_terms(refl, m_ref, c_ref):
    def step(k, carry):
        acc = [None, None]
        for r in range(RCV):
            rows = slice(8 * r, 8 * r + 8)
            mr, mi = m_ref[k, rows, 0:J], m_ref[k, rows, J : 2 * J]
            for s in range(2):
                rr, ri = both(refl, k, 2 * r + s)
                term = (rr * mr + ri * mi, rr * mi - ri * mr)
                acc[s] = term if acc[s] is None else cadd(acc[s], term)
        for s in range(2):
            c_ref[k, 8 * s : 8 * s + 8, 0:J] = acc[s][0]
            c_ref[k, 8 * s : 8 * s + 8, J : 2 * J] = acc[s][1]
        return carry

    lax.fori_loop(0, HALF, step, 0, unroll=True)


def window(onset, sample):
    return (sample >= BLOCKS * J // 2 - onset) & (sample <= BLOCKS * J // 2 - 1 + onset)


def middle(u_ref, a_ref, onset_ref, first, turn_ref, minus_ref):
    lane = lax.broadcasted_iota(jnp.int32, (8, J), 1)

    def step(pair, carry):
        kept = []
        for half in range(2):
            at = 2 * pair + half
            rows = pl.ds(pl.multiple_of(8 * at, 8), 8)
            mine = jnp.where(lane == first + at, onset_ref[...], 0).astype(F32)
            onset = jnp.broadcast_to(jnp.sum(mine, axis=1, keepdims=True), (8, J)).astype(jnp.int32)
            blocks = []
            for p, x in enumerate(load_blocks(turn_ref, 1, u_ref, rows)):
                blocks.append(jnp.where(window(onset, lane + p * J), x, 0.0).astype(BF16).astype(F32))
            kept.append(blocks)
            store_spectrum(turn_ref, blocks, a_ref, rows)
        for p in range(BLOCKS):
            joined = jnp.concatenate([kept[0][p], kept[1][p]], axis=0).astype(BF16)
            minus_ref[p, pl.ds(pl.multiple_of(16 * pair, 16), 16), :] = joined
        return carry

    lax.fori_loop(0, RCV // 2, step, 0)


def kernel(
    refl_ref, plus_ref, onset_r_ref, mat_hbm, turn_hbm,
    minus_out, parts, own_parts,
    refl, plus, mats, turns, onset_r,
    a_ref, hr_ref, hf_ref, u_ref, b_ref, m_ref, c_ref,
    minus, corr, peer, chip_sum,
    local_sem, one_sem, refl_sem, peer_sem,
):
    my_lag, my_src = lax.axis_index("lag"), lax.axis_index("src")
    chip, core = lax.div(my_lag, 2), lax.rem(my_lag, 2)

    def remote(source, target, send, recv, where):
        pltpu.make_async_remote_copy(
            src_ref=source, dst_ref=target, send_sem=send, recv_sem=recv, device_id=where, device_id_type=MESH
        ).start()

    def wait(ref, sem):
        pltpu.make_async_copy(ref, ref, sem).wait()

    loads = [
        (mat_hbm, mats), (turn_hbm, turns),
        (onset_r_ref.at[:, pl.ds(pl.multiple_of(my_src * J, J), J)], onset_r),
    ]
    loads = [pltpu.make_async_copy(a, b, local_sem.at[i]) for i, (a, b) in enumerate(loads)]
    for load in loads:
        load.start()

    barrier = pltpu.get_barrier_semaphore()

    def lag_at(i):
        return lax.rem(my_lag + i, LAGS)

    def src_at(d):
        return lax.rem(my_src + d, SRCS)

    def greet(lag, src):
        pl.semaphore_signal(barrier, inc=1, device_id=(lag, src), device_id_type=MESH)

    def greet_group(d, carry):
        for i in range(LAGS):
            greet(lag_at(i), src_at(d))
        return carry

    for i in range(1, LAGS):
        greet(lag_at(i), my_src)
    lax.fori_loop(1, SRCS, greet_group, 0)
    pl.semaphore_wait(barrier, LAGS * SRCS - 1)

    s_f, r_f, s_f2, r_f2, s_r, s_m, r_m, s_p, s_c, r_c, s_o, r_o = [one_sem.at[i] for i in range(12)]

    own = plus.at[core, my_src, chip]

    def same_core(i):
        return lax.rem(chip + i, CHIPS) * 2 + core

    def send_plus(d, carry):
        for i in range(CHIPS):
            remote(plus_ref, own, s_f, r_f, (same_core(i), src_at(d)))
        return carry

    def send_reflection(lag, src):
        remote(refl_ref.at[src, lag], refl.at[my_src, my_lag], s_r, refl_sem.at[my_src], (lag, src))

    def send_group(d, carry):
        for i in range(LAGS):
            send_reflection(lag_at(i), src_at(d))
        return carry

    for i in range(1, CHIPS):
        remote(plus_ref, own, s_f, r_f, (same_core(i), my_src))
    pltpu.make_async_copy(plus_ref, own, r_f).start()
    lax.fori_loop(1, SRCS, send_plus, 0)
    for i in range(1, LAGS):
        send_reflection(lag_at(i), my_src)
    pltpu.make_async_copy(refl_ref.at[my_src, my_lag], refl.at[my_src, my_lag], refl_sem.at[my_src]).start()
    lax.fori_loop(1, EARLY, send_group, 0)
    half = plus.at[core]
    other = chip * 2 + 1 - core
    wait(half, r_f)
    remote(half, half, s_f2, r_f2, (other, my_src))
    lax.fori_loop(EARLY, SRCS, send_group, 0)
    for load in loads:
        load.wait()
    u_ref[...] = jnp.zeros_like(u_ref)

    def source(d):
        return lax.rem(my_src + SRCS - d, SRCS)

    def reflection_spectra(groups):
        for g in groups:
            wait(refl.at[g], refl_sem.at[g])
        tiles = [lambda p, g=g: refl[g, p] for g in groups]
        transform(tiles, a_ref, [hr_ref.at[g] for g in groups], mats, turns)

    def early(i, carry):
        reflection_spectra([source(2 * i), source(2 * i + 1)])
        return carry

    lax.fori_loop(0, AHEAD // 2, early, 0)
    wait(half, r_f2)

    def plus_spectra(i, carry):
        tiles = [lambda p, g=g: plus[p % 2, g, p // 2] for g in (2 * i, 2 * i + 1)]
        transform(tiles, a_ref, [hf_ref.at[2 * i], hf_ref.at[2 * i + 1]], mats, turns)
        return carry

    lax.fori_loop(0, SRCS // 2, plus_spectra, 0)

    def forward(d, carry):
        g = source(d)
        pl.when(d >= AHEAD)(lambda: reflection_spectra([g]))
        forward_terms(hr_ref.at[g], hf_ref.at[g], u_ref)
        return carry

    lax.fori_loop(0, SRCS, forward, 0)
    u_ref[...] = product(u_ref[...], mats, 1)
    middle(u_ref, b_ref, onset_r, RCV * my_lag, turns, minus)

    def send_minus(i):
        remote(minus.at[lag_at(i)], minus_out.at[my_lag], s_m, r_m, (lag_at(i), my_src))

    pltpu.make_async_copy(minus.at[my_lag], minus_out.at[my_lag], r_m).start()
    for i in range(1, LAGS):
        send_minus(i)
    m_ref[...] = product(b_ref[...], mats, 0)

    def send_own():
        for i in range(1, LAGS):
            lag = lag_at(i)
            remote(corr.at[my_src, lax.rem(lag, 2), lax.div(lag, 2)], own_parts.at[my_lag], s_o, r_o, (lag, my_src))

    def add_and_send(g):
        wait(peer.at[g], peer_sem.at[g])
        chip_sum[g] = (corr[g, core].astype(F32) + peer[g].astype(F32)).astype(BF16)
        for i in range(CHIPS):
            to = lax.rem(chip + i, CHIPS)
            remote(chip_sum.at[g, to], parts.at[my_src, chip], s_c, r_c, (to * 2 + core, g))

    def partial_sums(groups):
        for h, g in enumerate(groups):
            backward_terms(hr_ref.at[g], m_ref, c_ref.at[pl.ds(h * HALF, HALF)])
        filled = slice(0, len(groups) * HALF)
        c_ref[filled] = product(c_ref[filled], mats, 2)
        for h, g in enumerate(groups):
            c_part = c_ref.at[pl.ds(h * HALF, HALF)]
            kept = [load_blocks(turns, 2, c_part, slice(8 * s, 8 * s + 8)) for s in range(2)]
            for p in range(BLOCKS):
                at = BLOCKS - 1 - p
                corr[g, p % 2, p // 2] = jnp.concatenate([kept[0][at], kept[1][at]], axis=0).astype(BF16)

    def to_other_core(g):
        remote(corr.at[g, 1 - core], peer.at[g], s_p, peer_sem.at[g], (other, my_src))

    def backward(i, carry):
        groups = [src_at(2 * i + 1), src_at(2 * i + 2)]
        partial_sums(groups)
        for g in groups:
            to_other_core(g)

        @pl.when(i > 0)
        def _():
            add_and_send(src_at(2 * i - 1))
            add_and_send(src_at(2 * i))

        return carry

    lax.fori_loop(0, SRCS // 2 - 1, backward, 0)
    partial_sums([src_at(SRCS - 1)])
    to_other_core(src_at(SRCS - 1))
    add_and_send(src_at(SRCS - 3))
    add_and_send(src_at(SRCS - 2))
    partial_sums([my_src])
    send_own()
    add_and_send(src_at(SRCS - 1))
    pltpu.make_async_copy(corr.at[my_src, core, chip], own_parts.at[my_lag], r_o).start()

    wait(parts.at[pl.ds(0, SRCS - 1)], r_c)
    wait(own_parts, r_o)
    wait(minus_out, r_m)
    wait(half.at[pl.ds(0, SRCS - 1)], s_f)
    wait(half.at[0, pl.ds(0, CHIPS - 1)], s_f)
    wait(half, s_f2)
    wait(refl.at[pl.ds(0, SRCS - 1)], s_r)
    wait(refl.at[0, pl.ds(0, LAGS - 1)], s_r)
    wait(minus_out.at[pl.ds(0, LAGS - 1)], s_m)
    wait(peer.at[pl.ds(0, SRCS - 1)], s_p)
    wait(parts.at[pl.ds(0, SRCS - 1)], s_c)
    wait(own_parts.at[pl.ds(0, LAGS - 1)], s_o)


def finish_kernel(minus_ref, parts, own_parts, start, onset_s, minus_out, next_out):
    my_lag, my_src = lax.axis_index("lag"), lax.axis_index("src")
    minus_out[...] = minus_ref[...]
    lane = lax.broadcasted_iota(jnp.int32, (8, J), 1)
    sums = [own_parts[l].astype(F32) for l in range(4)]
    for l in range(4, LAGS):
        sums[l % 4] = sums[l % 4] + own_parts[l].astype(F32)
    for d in range(1, SRCS):
        g = lax.rem(my_src + d, SRCS)
        for l in range(CHIPS):
            sums[l % 4] = sums[l % 4] + parts[g, l].astype(F32)
    total = (sums[0] + sums[1]) + (sums[2] + sums[3])
    begin = start[...].astype(F32)
    for s in range(2):
        row = jnp.broadcast_to(onset_s[s : s + 1, :], (8, 8)).astype(F32)
        pick = lax.broadcasted_iota(jnp.int32, (8, 8), 0) == lax.broadcasted_iota(jnp.int32, (8, 8), 1)
        onset = jnp.sum(jnp.where(pick, row, 0.0), axis=1, keepdims=True)
        mask = window(jnp.broadcast_to(onset, (8, J)).astype(jnp.int32), lane + my_lag * J)
        rows = slice(8 * s, 8 * s + 8)
        next_out[rows, :] = begin[rows] + jnp.where(mask, total[rows], 0.0)


def body(reflection, focus_plus, focus_start, onset_receiver, onset_source):
    vmem = pl.BlockSpec(memory_space=pltpu.VMEM)
    matrices, turns = tables()
    spectra = pltpu.VMEM((SRCS, HALF, 16, 2 * J), F32)
    tiles = pltpu.VMEM((SRCS, CHIPS, 16, J), BF16)
    minus_out, parts, own_parts = pl.pallas_call(
        kernel,
        out_shape=(
            jax.ShapeDtypeStruct((LAGS, 8 * RCV, J), BF16),
            jax.ShapeDtypeStruct((SRCS, CHIPS, 16, J), BF16),
            jax.ShapeDtypeStruct((LAGS, 16, J), BF16),
        ),
        in_specs=[pl.BlockSpec(memory_space=pl.ANY)] * 5,
        out_specs=(pl.BlockSpec(memory_space=pl.ANY),) * 3,
        scratch_shapes=[
            pltpu.VMEM((SRCS, LAGS, 16, J), BF16),
            pltpu.VMEM((2, SRCS, CHIPS, 16, J), BF16),
            pltpu.VMEM(matrices.shape, BF16),
            pltpu.VMEM(turns.shape, F32),
            pltpu.VMEM((8, J), jnp.int32),
            pltpu.VMEM((2 * HALF, 16, 2 * J), F32),
            spectra,
            spectra,
            pltpu.VMEM((HALF, 64, 2 * J), F32),
            pltpu.VMEM((HALF, 64, 2 * J), F32),
            pltpu.VMEM((HALF, 64, 2 * J), F32),
            pltpu.VMEM((2 * HALF, 16, 2 * J), F32),
            pltpu.VMEM((LAGS, 8 * RCV, J), BF16),
            pltpu.VMEM((SRCS, 2, CHIPS, 16, J), BF16),
            tiles,
            tiles,
            pltpu.SemaphoreType.DMA((3,)),
            pltpu.SemaphoreType.DMA((12,)),
            pltpu.SemaphoreType.DMA((SRCS,)),
            pltpu.SemaphoreType.DMA((SRCS,)),
        ],
        compiler_params=pltpu.CompilerParams(
            collective_id=0, has_side_effects=True, vmem_limit_bytes=60 * 2**20
        ),
        name="focus",
    )(
        reflection.reshape(SRCS, LAGS, 16, J),
        focus_plus.reshape(16, J),
        onset_receiver.T,
        jnp.asarray(matrices),
        jnp.asarray(turns),
    )
    minus_out, next_out = pl.pallas_call(
        finish_kernel,
        out_shape=(
            jax.ShapeDtypeStruct(minus_out.shape, BF16),
            jax.ShapeDtypeStruct((16, J), F32),
        ),
        in_specs=[vmem] * 5,
        out_specs=(vmem, vmem),
        name="finish",
    )(minus_out, parts, own_parts, focus_start.reshape(16, J), onset_source)
    return minus_out.reshape(J, 8, J), next_out.reshape(2, 8, J)


def solution(mesh):
    return jax.shard_map(
        body,
        mesh=mesh,
        in_specs=(
            P(None, "src", "lag"),
            P("src", None, "lag"),
            P("src", None, "lag"),
            P(),
            P("src", None),
        ),
        out_specs=(P("src", None, "lag"), P("src", None, "lag")),
        check_vma=False,
    )
```
